32 devices in a mesh: groups: 2 (over x), dict: 16 (over z, y, core).
Axes of the slice: x: 2, y: 2, z: 4, core: 2. Of those that a mesh axis runs over, the one named last changes fastest.
Arguments:
- tokens: bfloat16 [128, 4096], P(('groups', 'dict')), parts along dimension 0, may hold values from -25 to 25
- encoder_weight: bfloat16 [2624, 4096], P(('groups', 'dict')), parts along dimension 0, may hold values from -0.09375 to 0.09375
- encoder_bias: float32 [2624], P(('groups', 'dict')), parts along dimension 0, may hold values from -1 to 0.5
- decoder_weight: bfloat16 [2624, 4096], P(('groups', 'dict')), parts along dimension 0, may hold values from -0.15625 to 0.15625
- decoder_bias: float32 [8192], P('groups'), parts along dimension 0, may hold values from -3 to 3
- encoder_first: float32 [2624, 4096], P(('groups', 'dict')), parts along dimension 0, may hold values from -6 to 6
- encoder_second: float32 [2624, 4096], P(('groups', 'dict')), parts along dimension 0, may hold values from 1 to 100
- decoder_first: float32 [2624, 4096], P(('groups', 'dict')), parts along dimension 0, may hold values from -6 to 6
- decoder_second: float32 [2624, 4096], P(('groups', 'dict')), parts along dimension 0, may hold values from 1 to 100
- latent_first: float32 [2624], P(('groups', 'dict')), parts along dimension 0, may hold values from -6 to 6
- latent_second: float32 [2624], P(('groups', 'dict')), parts along dimension 0, may hold values from 1 to 100
- feature_first: float32 [8192], P('groups'), parts along dimension 0, may hold values from -6 to 6
- feature_second: float32 [8192], P('groups'), parts along dimension 0, may hold values from 10 to 1000
Outputs:
- new_encoder_weight: bfloat16 [2624, 4096], P(('groups', 'dict')), parts along dimension 0
- new_encoder_bias: float32 [2624], P(('groups', 'dict')), parts along dimension 0
- new_decoder_weight: bfloat16 [2624, 4096], P(('groups', 'dict')), parts along dimension 0
- new_decoder_bias: float32 [8192], P('groups'), parts along dimension 0
- new_encoder_first: float32 [2624, 4096], P(('groups', 'dict')), parts along dimension 0
- new_encoder_second: float32 [2624, 4096], P(('groups', 'dict')), parts along dimension 0
- new_decoder_first: float32 [2624, 4096], P(('groups', 'dict')), parts along dimension 0
- new_decoder_second: float32 [2624, 4096], P(('groups', 'dict')), parts along dimension 0
- new_latent_first: float32 [2624], P(('groups', 'dict')), parts along dimension 0
- new_latent_second: float32 [2624], P(('groups', 'dict')), parts along dimension 0
- new_feature_first: float32 [8192], P('groups'), parts along dimension 0
- new_feature_second: float32 [8192], P('groups'), parts along dimension 0
The draws below stay inside these ranges and needn't reach their ends.
There are 2 independent parts, one for each index of `groups`. The reference program is written for one: setup_inputs(seed, part) draws one part's arguments, and reference() takes and returns one part's arrays. A program takes and returns all parts, laid end to end along the dimension named above; each array names one. Nothing has to cross between parts.
All inputs are finite; a program needn't handle non-finite values.
Results may differ from the reference program's by a relative error of at most 0.0048.
Values may be sent and summed in bfloat16 or wider, within the bound.
No kernel may reach another device: no remote copies, remote signals or barrier semaphores. Data moves between devices by JAX's collectives and lax.ppermute only.
A program may use at most 128 MiB of HBM per device.

```python
import math
import jax
import jax.numpy as jnp
from jax import lax

D = 4096
STEP = 100
LATENTS = 1312
TOKENS = 64


def draw_tokens(key, part):
    key = jax.random.fold_in(key, 11)
    key_rows, key_vals = jax.random.split(key, 2)
    position = jnp.arange(TOKENS, dtype=jnp.float32) / max(TOKENS - 1, 1)
    rising = 3.0 ** position
    factor = jnp.exp(jax.random.uniform(key_rows, (TOKENS,), jnp.float32, -0.35, 0.35))
    values = jnp.clip(jax.random.normal(key_vals, (TOKENS, D), jnp.float32), -5.0, 5.0)
    return (values * (rising * factor)[:, None]).astype(jnp.bfloat16)


def level_of(own_key, shape, shards, low, top_value):
    def one(dim, blocks):
        draws = jax.random.uniform(jax.random.fold_in(jax.random.fold_in(own_key, 6), dim), (blocks,), jnp.float32, low / len(shards), top_value / len(shards))
        return jnp.repeat(jnp.exp(draws), shape[dim] // blocks).reshape((-1,) + (1,) * (len(shape) - dim - 1))

    level = one(*shards[0])
    for cut in shards[1:]:
        level = level * one(*cut)
    return level


def normal_values(stream_key, shape, width, limit, cuts=(), kind=jnp.bfloat16):
    loudness = level_of(stream_key, shape, cuts, -0.22, 0.18) if cuts else 1.0
    entries = jax.random.normal(stream_key, shape, jnp.float32) * width * loudness
    return jnp.minimum(jnp.maximum(entries, -limit), limit).astype(kind)


def setup_inputs(seed: int = 0, part: int = 0) -> dict:
    key_list = jax.random.split(jax.random.key(seed), 14)
    own_keys = jax.random.split(jax.random.fold_in(key_list[13], part), 14)
    tokens = draw_tokens(jax.random.fold_in(jax.random.fold_in(key_list[13], part), 71), part)
    encoder_weight = normal_values(own_keys[1], (LATENTS, D), D ** -0.5, 0.09375, ((0, 16),))
    encoder_bias = jnp.clip(-1.0 + 1.5 * jax.random.uniform(own_keys[2], (LATENTS,), jnp.float32) ** level_of(own_keys[2], (LATENTS,), ((0, 16),), -0.2, 0.2), -1.0, 0.5)
    decoder_weight = normal_values(own_keys[3], (LATENTS, D), LATENTS ** -0.5, 0.15625, ((0, 16),))
    decoder_bias = normal_values(own_keys[4], (D,), 0.5, 3.0, (), jnp.float32)
    encoder_first = normal_values(own_keys[5], (LATENTS, D), 1.0, 6.0, ((0, 16),), jnp.float32)
    encoder_second = jnp.clip(jnp.exp(math.log(100.0) - 4.6051702 * jax.random.uniform(own_keys[6], (LATENTS, D), jnp.float32) ** level_of(own_keys[6], (LATENTS, D), ((0, 16),), -0.2, 0.2)), 1.0, 100.0)
    decoder_first = normal_values(own_keys[7], (LATENTS, D), 1.0, 6.0, ((0, 16),), jnp.float32)
    decoder_second = jnp.clip(jnp.exp(math.log(100.0) - 4.6051702 * jax.random.uniform(own_keys[8], (LATENTS, D), jnp.float32) ** level_of(own_keys[8], (LATENTS, D), ((0, 16),), -0.2, 0.2)), 1.0, 100.0)
    latent_first = normal_values(own_keys[9], (LATENTS,), 1.0, 6.0, ((0, 16),), jnp.float32)
    latent_second = jnp.clip(jnp.exp(math.log(100.0) - 4.6051702 * jax.random.uniform(own_keys[10], (LATENTS,), jnp.float32) ** level_of(own_keys[10], (LATENTS,), ((0, 16),), -0.2, 0.2)), 1.0, 100.0)
    feature_first = normal_values(own_keys[11], (D,), 1.0, 6.0, (), jnp.float32)
    feature_second = jnp.clip(jnp.exp(jax.random.uniform(own_keys[12], (D,), jnp.float32, math.log(10.0), math.log(1000.0))), 10.0, 1000.0)
    return dict(tokens=tokens, encoder_weight=encoder_weight, encoder_bias=encoder_bias, decoder_weight=decoder_weight, decoder_bias=decoder_bias, encoder_first=encoder_first, encoder_second=encoder_second, decoder_first=decoder_first, decoder_second=decoder_second, latent_first=latent_first, latent_second=latent_second, feature_first=feature_first, feature_second=feature_second)


sharpness = 4.0
sparsity_coef = 0.3
first_decay = 0.9
second_decay = 0.999
learn_rate = 0.001
epsilon = 1e-08

def adam_update(param, grad, first, second):
    first_new = first_decay * first + (1.0 - first_decay) * grad
    second_new = second_decay * second + (1.0 - second_decay) * grad * grad
    first_corr = 1.0 - first_decay ** STEP
    second_corr = 1.0 - second_decay ** STEP
    change = learn_rate * (first_new / first_corr) / (jnp.sqrt(second_new / second_corr) + epsilon)
    return (param.astype(jnp.float32) - change, first_new, second_new)

def reference(tokens, encoder_weight, encoder_bias, decoder_weight, decoder_bias, encoder_first, encoder_second, decoder_first, decoder_second, latent_first, latent_second, feature_first, feature_second):
    pre = jnp.dot(tokens, encoder_weight.T, preferred_element_type=jnp.float32) + encoder_bias
    act = jax.nn.softplus(sharpness * pre) / sharpness
    act_low = act.astype(jnp.bfloat16)
    recon = jnp.dot(act_low, decoder_weight, preferred_element_type=jnp.float32)
    errors = (recon + decoder_bias - tokens.astype(jnp.float32)).astype(jnp.bfloat16)
    decoder_full = decoder_weight.astype(jnp.float32)
    norms = jnp.sqrt(lax.optimization_barrier(jnp.sum(decoder_full * decoder_full, axis=1)) + 1e-06)
    act_total = lax.optimization_barrier(jnp.sum(act, axis=0))
    decoder_grad = jnp.dot(act_low.T, errors, preferred_element_type=jnp.float32)
    decoder_grad = decoder_grad + sparsity_coef * act_total[:, None] * decoder_full / norms[:, None]
    act_grad = jnp.dot(errors, decoder_weight.T, preferred_element_type=jnp.float32) + sparsity_coef * norms
    pre_grad = act_grad * jax.nn.sigmoid(sharpness * pre)
    latent_grad = lax.optimization_barrier(jnp.sum(pre_grad, axis=0))
    pre_low = pre_grad.astype(jnp.bfloat16)
    encoder_grad = jnp.dot(pre_low.T, tokens, preferred_element_type=jnp.float32)
    feature_grad = lax.optimization_barrier(jnp.sum(errors.astype(jnp.float32), axis=0))
    enc_new, enc_first, enc_second = adam_update(encoder_weight, encoder_grad, encoder_first, encoder_second)
    lat_new, lat_first, lat_second = adam_update(encoder_bias, latent_grad, latent_first, latent_second)
    dec_new, dec_first, dec_second = adam_update(decoder_weight, decoder_grad, decoder_first, decoder_second)
    feat_new, feat_first, feat_second = adam_update(decoder_bias, feature_grad, feature_first, feature_second)
    return (enc_new.astype(jnp.bfloat16), lat_new, dec_new.astype(jnp.bfloat16), feat_new, enc_first, enc_second, dec_first, dec_second, lat_first, lat_second, feat_first, feat_second)
```

```python
import jax
import jax.numpy as jnp
from jax import lax
from jax.sharding import PartitionSpec as P

STEP = 100


sharpness = 4.0
sparsity_coef = 0.3
first_decay = 0.9
second_decay = 0.999
learn_rate = 0.001
epsilon = 1e-08


def adam_update(param, grad, first, second):
    first_new = first_decay * first + (1.0 - first_decay) * grad
    second_new = second_decay * second + (1.0 - second_decay) * grad * grad
    first_corr = 1.0 - first_decay**STEP
    second_corr = 1.0 - second_decay**STEP
    change = learn_rate * (first_new / first_corr) / (jnp.sqrt(second_new / second_corr) + epsilon)
    return (param.astype(jnp.float32) - change, first_new, second_new)


def swap(x, bit, devices):
    return lax.ppermute(x, "dict", [(i, i ^ bit) for i in range(devices)])


def local(
    devices,
    tokens,
    encoder_weight,
    encoder_bias,
    decoder_weight,
    decoder_bias,
    encoder_first,
    encoder_second,
    decoder_first,
    decoder_second,
    latent_first,
    latent_second,
    feature_first,
    feature_second,
):
    bits = [1 << b for b in reversed(range(devices.bit_length() - 1))]
    own = tokens.shape[0]
    gathered = tokens
    for bit in bits:
        gathered = jnp.concatenate([gathered, swap(gathered, bit, devices)], axis=0)
    pre = (
        jnp.einsum("td,ld->tl", gathered, encoder_weight, preferred_element_type=jnp.float32)
        + encoder_bias
    )
    act = jax.nn.softplus(sharpness * pre) / sharpness
    act_low = act.astype(jnp.bfloat16)
    part = jnp.dot(act_low, decoder_weight, preferred_element_type=jnp.float32)
    for bit in reversed(bits[1:]):
        half = part.shape[0] // 2
        part = part[:half] + swap(part[half:].astype(jnp.bfloat16), bit, devices).astype(jnp.float32)
    part = lax.reduce_precision(part, 8, 7)
    other = swap(part.astype(jnp.bfloat16), bits[0], devices).astype(jnp.float32)
    recon = part + jnp.concatenate([other[own:], other[:own]], axis=0)
    errors = (recon + decoder_bias - gathered[: 2 * own].astype(jnp.float32)).astype(jnp.bfloat16)
    for bit in bits[1:]:
        errors = jnp.concatenate([errors, swap(errors, bit, devices)], axis=0)
    rows = errors.astype(jnp.float32).reshape(devices, own, -1)
    feature_grad = rows[:, 0]
    for row in range(1, own):
        feature_grad = feature_grad + rows[:, row]
    while feature_grad.shape[0] > 1:
        half = feature_grad.shape[0] // 2
        feature_grad = feature_grad[:half] + feature_grad[half:]
    feature_grad = feature_grad[0]
    decoder_full = decoder_weight.astype(jnp.float32)
    norms = jnp.sqrt(jnp.sum(decoder_full * decoder_full, axis=1) + 1e-06)
    act_total = jnp.sum(act, axis=0)
    decoder_grad = jnp.einsum("tl,td->ld", act_low, errors, preferred_element_type=jnp.float32)
    decoder_grad = decoder_grad + sparsity_coef * act_total[:, None] * decoder_full / norms[:, None]
    act_grad = (
        jnp.einsum("td,ld->tl", errors, decoder_weight, preferred_element_type=jnp.float32)
        + sparsity_coef * norms
    )
    pre_grad = act_grad * jax.nn.sigmoid(sharpness * pre)
    latent_grad = jnp.sum(pre_grad, axis=0)
    pre_low = pre_grad.astype(jnp.bfloat16)
    encoder_grad = jnp.einsum("tl,td->ld", pre_low, gathered, preferred_element_type=jnp.float32)
    enc_new, enc_first, enc_second = adam_update(
        encoder_weight, encoder_grad, encoder_first, encoder_second
    )
    lat_new, lat_first, lat_second = adam_update(
        encoder_bias, latent_grad, latent_first, latent_second
    )
    dec_new, dec_first, dec_second = adam_update(
        decoder_weight, decoder_grad, decoder_first, decoder_second
    )
    feat_new, feat_first, feat_second = adam_update(
        decoder_bias, feature_grad, feature_first, feature_second
    )
    return (
        enc_new.astype(jnp.bfloat16),
        lat_new,
        dec_new.astype(jnp.bfloat16),
        feat_new,
        enc_first,
        enc_second,
        dec_first,
        dec_second,
        lat_first,
        lat_second,
        feat_first,
        feat_second,
    )


def solution(mesh):
    devices = mesh.shape["dict"]
    in_specs = (
        P(("groups", "dict"), None),
        P(("groups", "dict"), None),
        P(("groups", "dict")),
        P(("groups", "dict"), None),
        P("groups"),
        P(("groups", "dict"), None),
        P(("groups", "dict"), None),
        P(("groups", "dict"), None),
        P(("groups", "dict"), None),
        P(("groups", "dict")),
        P(("groups", "dict")),
        P("groups"),
        P("groups"),
    )
    out_specs = (
        P(("groups", "dict"), None),
        P(("groups", "dict")),
        P(("groups", "dict"), None),
        P("groups"),
        P(("groups", "dict"), None),
        P(("groups", "dict"), None),
        P(("groups", "dict"), None),
        P(("groups", "dict"), None),
        P(("groups", "dict")),
        P(("groups", "dict")),
        P("groups"),
        P("groups"),
    )

    def step(*args):
        return local(devices, *args)

    return jax.shard_map(step, mesh=mesh, in_specs=in_specs, out_specs=out_specs, check_vma=False)
```

```python
import jax
import jax.numpy as jnp
from jax import lax
from jax.sharding import PartitionSpec as P

STEP = 100


sharpness = 4.0
sparsity_coef = 0.3
first_decay = 0.9
second_decay = 0.999
learn_rate = 0.001
epsilon = 1e-08


def adam_update(param, grad, first, second):
    first_new = first_decay * first + (1.0 - first_decay) * grad
    second_new = second_decay * second + (1.0 - second_decay) * grad * grad
    first_corr = 1.0 - first_decay**STEP
    second_corr = 1.0 - second_decay**STEP
    change = learn_rate * (first_new / first_corr) / (jnp.sqrt(second_new / second_corr) + epsilon)
    return (param.astype(jnp.float32) - change, first_new, second_new)


def swap(x, bit, devices):
    return lax.ppermute(x, "dict", [(i, i ^ bit) for i in range(devices)])


def activation(tokens, weight, bias):
    pre = jnp.einsum("td,ld->tl", tokens, weight, preferred_element_type=jnp.float32) + bias
    return pre, jax.nn.softplus(sharpness * pre) / sharpness


def local(
    devices,
    tokens,
    encoder_weight,
    encoder_bias,
    decoder_weight,
    decoder_bias,
    encoder_first,
    encoder_second,
    decoder_first,
    decoder_second,
    latent_first,
    latent_second,
    feature_first,
    feature_second,
):
    bits = [1 << b for b in reversed(range(1, devices.bit_length() - 1))]
    own = tokens.shape[0]
    mate_encoder = swap(encoder_weight, 1, devices)
    mate_bias = swap(encoder_bias, 1, devices)
    mate_decoder = swap(decoder_weight, 1, devices)
    column = tokens
    for bit in bits:
        column = lax.optimization_barrier(jnp.concatenate([column, swap(column, bit, devices)], axis=0))
    part = jnp.dot(
        activation(column, encoder_weight, encoder_bias)[1].astype(jnp.bfloat16),
        decoder_weight,
        preferred_element_type=jnp.float32,
    ) + jnp.dot(
        activation(column, mate_encoder, mate_bias)[1].astype(jnp.bfloat16),
        mate_decoder,
        preferred_element_type=jnp.float32,
    )
    half = part.shape[0] // 2
    part = part[:half] + swap(part[half:].astype(jnp.bfloat16), bits[-1], devices).astype(jnp.float32)
    for level in reversed(range(len(bits) - 1)):
        part = lax.reduce_precision(part, 8, 7)
        other = swap(part.astype(jnp.bfloat16), bits[level], devices).astype(jnp.float32)
        other = other.reshape(-1, 2, own << level, other.shape[-1])
        part = part + other[:, ::-1].reshape(part.shape)
    errors = (part + decoder_bias - column[:half].astype(jnp.float32)).astype(jnp.bfloat16)
    errors = lax.optimization_barrier(jnp.concatenate([errors, swap(errors, bits[-1], devices)], axis=0))
    errors = lax.optimization_barrier(jnp.concatenate([errors, swap(errors, 1, devices)], axis=0))
    gathered = jnp.concatenate([column, swap(column, 1, devices)], axis=0)
    pre, act = activation(gathered, encoder_weight, encoder_bias)
    act_low = act.astype(jnp.bfloat16)
    rows = errors.astype(jnp.float32).reshape(devices, own, -1)
    feature_grad = rows[:, 0]
    for row in range(1, own):
        feature_grad = feature_grad + rows[:, row]
    while feature_grad.shape[0] > 1:
        half = feature_grad.shape[0] // 2
        feature_grad = feature_grad[:half] + feature_grad[half:]
    feature_grad = feature_grad[0]
    decoder_full = decoder_weight.astype(jnp.float32)
    norms = jnp.sqrt(jnp.sum(decoder_full * decoder_full, axis=1) + 1e-06)
    act_total = jnp.sum(act, axis=0)
    decoder_grad = jnp.einsum("tl,td->ld", act_low, errors, preferred_element_type=jnp.float32)
    decoder_grad = decoder_grad + sparsity_coef * act_total[:, None] * decoder_full / norms[:, None]
    act_grad = (
        jnp.einsum("td,ld->tl", errors, decoder_weight, preferred_element_type=jnp.float32)
        + sparsity_coef * norms
    )
    pre_grad = act_grad * jax.nn.sigmoid(sharpness * pre)
    latent_grad = jnp.sum(pre_grad, axis=0)
    pre_low = pre_grad.astype(jnp.bfloat16)
    encoder_grad = jnp.einsum("tl,td->ld", pre_low, gathered, preferred_element_type=jnp.float32)
    enc_new, enc_first, enc_second = adam_update(
        encoder_weight, encoder_grad, encoder_first, encoder_second
    )
    lat_new, lat_first, lat_second = adam_update(
        encoder_bias, latent_grad, latent_first, latent_second
    )
    dec_new, dec_first, dec_second = adam_update(
        decoder_weight, decoder_grad, decoder_first, decoder_second
    )
    feat_new, feat_first, feat_second = adam_update(
        decoder_bias, feature_grad, feature_first, feature_second
    )
    return (
        enc_new.astype(jnp.bfloat16),
        lat_new,
        dec_new.astype(jnp.bfloat16),
        feat_new,
        enc_first,
        enc_second,
        dec_first,
        dec_second,
        lat_first,
        lat_second,
        feat_first,
        feat_second,
    )


def solution(mesh):
    devices = mesh.shape["dict"]
    in_specs = (
        P(("groups", "dict"), None),
        P(("groups", "dict"), None),
        P(("groups", "dict")),
        P(("groups", "dict"), None),
        P("groups"),
        P(("groups", "dict"), None),
        P(("groups", "dict"), None),
        P(("groups", "dict"), None),
        P(("groups", "dict"), None),
        P(("groups", "dict")),
        P(("groups", "dict")),
        P("groups"),
        P("groups"),
    )
    out_specs = (
        P(("groups", "dict"), None),
        P(("groups", "dict")),
        P(("groups", "dict"), None),
        P("groups"),
        P(("groups", "dict"), None),
        P(("groups", "dict"), None),
        P(("groups", "dict"), None),
        P(("groups", "dict"), None),
        P(("groups", "dict")),
        P(("groups", "dict")),
        P("groups"),
        P("groups"),
    )

    def step(*args):
        return local(devices, *args)

    return jax.shard_map(step, mesh=mesh, in_specs=in_specs, out_specs=out_specs, check_vma=False)
```

```python
import functools

import jax
import jax.numpy as jnp
from jax import lax
from jax.experimental import pallas as pl
from jax.experimental.pallas import tpu as pltpu
from jax.sharding import PartitionSpec as P

STEP = 100


sharpness = 4.0
sparsity_coef = 0.3
first_decay = 0.9
second_decay = 0.999
learn_rate = 0.001
epsilon = 1e-08

f32 = jnp.float32
bf16 = jnp.bfloat16


def adam_update(param, grad, first, second):
    first_new = first_decay * first + (1.0 - first_decay) * grad
    second_new = second_decay * second + (1.0 - second_decay) * grad * grad
    first_corr = 1.0 - first_decay**STEP
    second_corr = 1.0 - second_decay**STEP
    square = second_new * (1.0 / second_corr)
    root = square * lax.rsqrt(square)
    change = (learn_rate / first_corr) * first_new / (root + epsilon)
    return (param.astype(f32) - change, first_new, second_new)


def softplus(x):
    return jnp.maximum(x, 0.0) + jnp.log1p(jnp.exp(-jnp.abs(x)))


def nt_dot(a, b):
    return lax.dot_general(a, b, (((1,), (1,)), ((), ())), preferred_element_type=f32)


def turn(vector):
    side = max(vector.shape)
    square = (side, side)
    diagonal = lax.broadcasted_iota(jnp.int32, square, 0) == lax.broadcasted_iota(jnp.int32, square, 1)
    axis = 1 if vector.shape[0] == 1 else 0
    return jnp.sum(jnp.where(diagonal, jnp.broadcast_to(vector, square), 0.0), axis=axis, keepdims=True)


def swap(x, bit, devices):
    return lax.ppermute(x, "dict", [(i, i ^ bit) for i in range(devices)])


def in_vmem(array):
    return pltpu.with_memory_space_constraint(array, pltpu.VMEM)


def in_hbm(array):
    return pltpu.with_memory_space_constraint(array, pltpu.HBM)


VMEM_SPEC = pl.BlockSpec(memory_space=pltpu.VMEM)
ANY_SPEC = pl.BlockSpec(memory_space=pl.ANY)


def load_kernel(*refs):
    count = len(refs) // 2
    copies = [pltpu.make_async_copy(refs[i], refs[count + i], refs[-1].at[i]) for i in range(count)]
    for copy in copies:
        copy.start()
    for copy in copies:
        copy.wait()


def load(*arrays):
    return pl.pallas_call(
        load_kernel,
        in_specs=[ANY_SPEC] * len(arrays),
        out_specs=[VMEM_SPEC] * len(arrays),
        out_shape=[pltpu.VMEM(array.shape, array.dtype) for array in arrays],
        scratch_shapes=[pltpu.SemaphoreType.DMA((len(arrays),))],
        compiler_params=pltpu.CompilerParams(vmem_limit_bytes=2**20),
        cost_estimate=pl.CostEstimate(
            flops=0, bytes_accessed=2 * sum(array.size * array.dtype.itemsize for array in arrays), transcendentals=0
        ),
    )(*map(in_hbm, arrays))


def forward_kernel(
    tokens_ref, encoder_ref, mate_encoder_ref, bias_ref, mate_bias_ref, decoder_ref, mate_decoder_ref, keep_ref, send_ref
):
    tokens = tokens_ref[...]

    def act(weight_ref, row_ref):
        pre = nt_dot(tokens, weight_ref[...]) + row_ref[...]
        return (softplus(sharpness * pre) / sharpness).astype(bf16)

    own = act(encoder_ref, bias_ref)
    mate = act(mate_encoder_ref, mate_bias_ref)
    half = keep_ref.shape[0]
    width = 1024
    for start in range(0, keep_ref.shape[1], width):
        columns = pl.ds(start, width)
        part = jnp.dot(own, decoder_ref[:, columns], preferred_element_type=f32) + jnp.dot(
            mate, mate_decoder_ref[:, columns], preferred_element_type=f32
        )
        keep_ref[:, columns] = part[:half]
        send_ref[:, columns] = part[half:].astype(bf16)


def forward(tokens, encoder, mate_encoder, bias, mate_bias, decoder, mate_decoder):
    half, features = tokens.shape[0] // 2, tokens.shape[1]
    latents = encoder.shape[0]
    return pl.pallas_call(
        forward_kernel,
        in_specs=[VMEM_SPEC] * 7,
        out_specs=[VMEM_SPEC] * 2,
        out_shape=[pltpu.VMEM((half, features), f32), pltpu.VMEM((half, features), bf16)],
        compiler_params=pltpu.CompilerParams(vmem_limit_bytes=16 * 2**20),
        cost_estimate=pl.CostEstimate(
            flops=16 * half * latents * features, bytes_accessed=8 * latents * features, transcendentals=8 * half * latents
        ),
    )(*map(in_vmem, (tokens, encoder, mate_encoder, bias, mate_bias, decoder, mate_decoder)))


def prepare_kernel(
    tokens_ref,
    mate_tokens_ref,
    encoder_ref,
    bias_ref,
    decoder_ref,
    encoder_first_ref,
    encoder_second_ref,
    decoder_first_ref,
    decoder_second_ref,
    gathered_ref,
    slope_ref,
    act_ref,
    floor_ref,
    pull_ref,
    encoder_first_out,
    encoder_second_out,
    decoder_first_out,
    decoder_second_out,
    sems,
):
    moves = [
        (encoder_first_ref, encoder_first_out),
        (encoder_second_ref, encoder_second_out),
        (decoder_first_ref, decoder_first_out),
        (decoder_second_ref, decoder_second_out),
    ]
    pieces = sems.shape[1]
    width = encoder_first_ref.shape[1] // pieces
    copies = [
        pltpu.make_async_copy(
            source.at[:, pl.ds(piece * width, width)], target.at[:, pl.ds(piece * width, width)], sems.at[which, piece]
        )
        for which, (source, target) in enumerate(moves)
        for piece in range(pieces)
    ]
    for copy in copies:
        copy.start()
    tokens = jnp.concatenate([tokens_ref[...], mate_tokens_ref[...]], axis=0)
    gathered_ref[...] = tokens
    pre = nt_dot(encoder_ref[...], tokens) + turn(bias_ref[...])
    act = softplus(sharpness * pre) / sharpness
    slope_ref[...] = jax.nn.sigmoid(sharpness * pre)
    act_ref[...] = act.astype(bf16)
    decoder = decoder_ref[...].astype(f32)
    norms = jnp.sqrt(jnp.sum(decoder * decoder, axis=1, keepdims=True) + 1e-06)
    floor_ref[...] = sparsity_coef * norms
    pull_ref[...] = sparsity_coef * jnp.sum(act, axis=1, keepdims=True) / norms
    for copy in copies:
        copy.wait()


def prepare(tokens, mate_tokens, encoder, bias, decoder, *moments):
    latents, features = encoder.shape
    count = 2 * tokens.shape[0]
    return pl.pallas_call(
        prepare_kernel,
        in_specs=[VMEM_SPEC] * 5 + [ANY_SPEC] * 4,
        out_specs=[VMEM_SPEC] * 9,
        out_shape=[
            pltpu.VMEM((count, features), bf16),
            pltpu.VMEM((latents, count), f32),
            pltpu.VMEM((latents, count), bf16),
            pltpu.VMEM((latents, 1), f32),
            pltpu.VMEM((latents, 1), f32),
        ]
        + [pltpu.VMEM((latents, features), f32)] * 4,
        scratch_shapes=[pltpu.SemaphoreType.DMA((4, 2))],
        compiler_params=pltpu.CompilerParams(vmem_limit_bytes=16 * 2**20),
        cost_estimate=pl.CostEstimate(
            flops=2 * count * latents * features, bytes_accessed=20 * latents * features, transcendentals=3 * count * latents
        ),
    )(*map(in_vmem, (tokens, mate_tokens, encoder, bias, decoder)), *map(in_hbm, moments))


def update_kernel(
    own,
    errors_ref,
    tokens_ref,
    slope_ref,
    act_ref,
    floor_ref,
    pull_ref,
    encoder_first_ref,
    encoder_second_ref,
    decoder_first_ref,
    decoder_second_ref,
    encoder_ref,
    decoder_ref,
    encoder_bias_ref,
    latent_first_ref,
    latent_second_ref,
    decoder_bias_ref,
    feature_first_ref,
    feature_second_ref,
    *refs,
):
    outs, slots, (pre_ref, sems) = refs[:12], refs[12:24], refs[24:]
    features = encoder_ref.shape[1]
    blocks = sems.shape[1]
    width = features // blocks

    def block_copy(which, block):
        columns = pl.ds(pl.multiple_of(block * width, width), width)
        return pltpu.make_async_copy(slots[which].at[:, columns], outs[which].at[:, columns], sems.at[which, block])

    def whole_copy(which):
        return pltpu.make_async_copy(slots[which], outs[which], sems.at[which, 0])

    def decoder_block(block, carry):
        columns = pl.ds(pl.multiple_of(block * width, width), width)
        weight = decoder_ref[:, columns].astype(f32)
        grad = jnp.dot(act_ref[...], errors_ref[:, columns], preferred_element_type=f32) + pull_ref[...] * weight
        new, slots[4][:, columns], slots[5][:, columns] = adam_update(
            weight, grad, decoder_first_ref[:, columns], decoder_second_ref[:, columns]
        )
        slots[1][:, columns] = new.astype(bf16)
        for which in (1, 4, 5):
            block_copy(which, block).start()
        return carry

    lax.fori_loop(0, blocks, decoder_block, 0)

    grad = (nt_dot(decoder_ref[...], errors_ref[...]) + floor_ref[...]) * slope_ref[...]
    pre_ref[...] = grad.astype(bf16)
    total = turn(jnp.sum(grad, axis=1, keepdims=True))
    slots[6][...], slots[7][...], slots[8][...] = adam_update(
        encoder_bias_ref[...], total, latent_first_ref[...], latent_second_ref[...]
    )
    rows = errors_ref[...].astype(f32)
    while rows.shape[0] > own:
        half = rows.shape[0] // 2
        rows = rows[:half] + rows[half:]
    total = rows[0:1]
    for row in range(1, own):
        total = total + rows[row : row + 1]
    slots[9][...], slots[10][...], slots[11][...] = adam_update(
        decoder_bias_ref[...], total, feature_first_ref[...], feature_second_ref[...]
    )
    for which in range(6, 12):
        whole_copy(which).start()

    def encoder_block(block, carry):
        columns = pl.ds(pl.multiple_of(block * width, width), width)
        grad = jnp.dot(pre_ref[...], tokens_ref[:, columns], preferred_element_type=f32)
        new, slots[2][:, columns], slots[3][:, columns] = adam_update(
            encoder_ref[:, columns], grad, encoder_first_ref[:, columns], encoder_second_ref[:, columns]
        )
        slots[0][:, columns] = new.astype(bf16)
        for which in (0, 2, 3):
            block_copy(which, block).start()
        return carry

    lax.fori_loop(0, blocks, encoder_block, 0)
    for block in range(blocks):
        for which in range(6):
            block_copy(which, block).wait()
    for which in range(6, 12):
        whole_copy(which).wait()


def update(own, errors, prepared, encoder, decoder, *short):
    latents, features = encoder.shape
    count = errors.shape[0]
    shapes = [((latents, features), bf16)] * 2 + [((latents, features), f32)] * 4
    shapes += [((1, latents), f32)] * 3 + [((1, features), f32)] * 3
    return pl.pallas_call(
        functools.partial(update_kernel, own),
        in_specs=[VMEM_SPEC] * 18,
        out_specs=[ANY_SPEC] * 12,
        out_shape=[jax.ShapeDtypeStruct(*shape) for shape in shapes],
        scratch_shapes=[pltpu.VMEM(*shape) for shape in shapes]
        + [pltpu.VMEM((latents, count), bf16), pltpu.SemaphoreType.DMA((12, 8))],
        compiler_params=pltpu.CompilerParams(vmem_limit_bytes=24 * 2**20),
        cost_estimate=pl.CostEstimate(
            flops=6 * count * latents * features,
            bytes_accessed=40 * latents * features,
            transcendentals=4 * latents * features,
        ),
    )(*map(in_vmem, (errors, *prepared, encoder, decoder, *short)))


def local(
    devices,
    tokens,
    encoder_weight,
    encoder_bias,
    decoder_weight,
    decoder_bias,
    encoder_first,
    encoder_second,
    decoder_first,
    decoder_second,
    latent_first,
    latent_second,
    feature_first,
    feature_second,
):
    bits = [1 << b for b in reversed(range(1, devices.bit_length() - 1))]
    own = tokens.shape[0]
    row = lambda array: array.reshape(1, -1)
    encoder_bias, latent_first, latent_second, decoder_bias, feature_first, feature_second = map(
        row, (encoder_bias, latent_first, latent_second, decoder_bias, feature_first, feature_second)
    )
    far = swap(tokens, bits[0], devices)
    column, encoder, decoder, bias = load(tokens, encoder_weight, decoder_weight, encoder_bias)
    column = lax.optimization_barrier(jnp.concatenate([column, far], axis=0))
    mate_encoder = swap(encoder, 1, devices)
    mate_bias = swap(bias, 1, devices)
    mate_decoder = swap(decoder, 1, devices)
    for bit in bits[1:]:
        column = lax.optimization_barrier(jnp.concatenate([column, swap(column, bit, devices)], axis=0))
    part, send = forward(column, encoder, mate_encoder, bias, mate_bias, decoder, mate_decoder)
    part = part + swap(send, bits[-1], devices).astype(f32)
    mate_column = swap(column, 1, devices)
    half = part.shape[0]
    for level in reversed(range(len(bits) - 1)):
        part = lax.reduce_precision(part, 8, 7)
        sent = part.astype(bf16)
        if level == 0:
            sent, mate_column = lax.optimization_barrier((sent, mate_column))
        other = swap(sent, bits[level], devices)
        if level == 0:
            prepared = prepare(
                column, mate_column, encoder, bias, decoder, encoder_first, encoder_second, decoder_first, decoder_second
            )
            other, prepared = lax.optimization_barrier((other, prepared))
        size = own << level
        pieces = [other[start ^ size : (start ^ size) + size] for start in range(0, half, size)]
        part = part + jnp.concatenate(pieces, axis=0).astype(f32)
    errors = (part + decoder_bias - column[:half].astype(f32)).astype(bf16)
    errors = lax.optimization_barrier(jnp.concatenate([errors, swap(errors, bits[-1], devices)], axis=0))
    errors = jnp.concatenate([errors, swap(errors, 1, devices)], axis=0)
    out = update(
        own,
        errors,
        prepared,
        encoder,
        decoder,
        bias,
        latent_first,
        latent_second,
        decoder_bias,
        feature_first,
        feature_second,
    )
    new_encoder, new_decoder, enc_first, enc_second, dec_first, dec_second = out[:6]
    lat_new, lat_first, lat_second, feat_new, feat_first, feat_second = (array.reshape(-1) for array in out[6:])
    return (
        new_encoder,
        lat_new,
        new_decoder,
        feat_new,
        enc_first,
        enc_second,
        dec_first,
        dec_second,
        lat_first,
        lat_second,
        feat_first,
        feat_second,
    )


def solution(mesh):
    devices = mesh.shape["dict"]
    in_specs = (
        P(("groups", "dict"), None),
        P(("groups", "dict"), None),
        P(("groups", "dict")),
        P(("groups", "dict"), None),
        P("groups"),
        P(("groups", "dict"), None),
        P(("groups", "dict"), None),
        P(("groups", "dict"), None),
        P(("groups", "dict"), None),
        P(("groups", "dict")),
        P(("groups", "dict")),
        P("groups"),
        P("groups"),
    )
    out_specs = (
        P(("groups", "dict"), None),
        P(("groups", "dict")),
        P(("groups", "dict"), None),
        P("groups"),
        P(("groups", "dict"), None),
        P(("groups", "dict"), None),
        P(("groups", "dict"), None),
        P(("groups", "dict"), None),
        P(("groups", "dict")),
        P(("groups", "dict")),
        P("groups"),
        P("groups"),
    )

    def step(*args):
        return local(devices, *args)

    return jax.shard_map(step, mesh=mesh, in_specs=in_specs, out_specs=out_specs, check_vma=False)
```

```python
import functools

import jax
import jax.numpy as jnp
from jax import lax
from jax.experimental import pallas as pl
from jax.experimental.pallas import tpu as pltpu
from jax.sharding import PartitionSpec as P

STEP = 100


sharpness = 4.0
sparsity_coef = 0.3
first_decay = 0.9
second_decay = 0.999
learn_rate = 0.001
epsilon = 1e-08

f32 = jnp.float32
bf16 = jnp.bfloat16


def adam_update(param, grad, first, second):
    first_new = first_decay * first + (1.0 - first_decay) * grad
    second_new = second_decay * second + (1.0 - second_decay) * grad * grad
    first_corr = 1.0 - first_decay**STEP
    second_corr = 1.0 - second_decay**STEP
    square = second_new * (1.0 / second_corr)
    root = square * lax.rsqrt(square)
    change = (learn_rate / first_corr) * first_new / (root + epsilon)
    return (param.astype(f32) - change, first_new, second_new)


def softplus(x):
    return jnp.maximum(x, 0.0) + jnp.log1p(jnp.exp(-jnp.abs(x)))


def nt_dot(a, b):
    return lax.dot_general(a, b, (((1,), (1,)), ((), ())), preferred_element_type=f32)


def turn(vector):
    side = max(vector.shape)
    square = (side, side)
    diagonal = lax.broadcasted_iota(jnp.int32, square, 0) == lax.broadcasted_iota(jnp.int32, square, 1)
    axis = 1 if vector.shape[0] == 1 else 0
    return jnp.sum(jnp.where(diagonal, jnp.broadcast_to(vector, square), 0.0), axis=axis, keepdims=True)


def swap(x, bit, devices):
    return lax.ppermute(x, "dict", [(i, i ^ bit) for i in range(devices)])


def in_vmem(array):
    return pltpu.with_memory_space_constraint(array, pltpu.VMEM)


def in_hbm(array):
    return pltpu.with_memory_space_constraint(array, pltpu.HBM)


VMEM_SPEC = pl.BlockSpec(memory_space=pltpu.VMEM)
ANY_SPEC = pl.BlockSpec(memory_space=pl.ANY)


def load_kernel(*refs):
    count = len(refs) // 2
    copies = [pltpu.make_async_copy(refs[i], refs[count + i], refs[-1].at[i]) for i in range(count)]
    for copy in copies:
        copy.start()
    for copy in copies:
        copy.wait()


def load(*arrays):
    return pl.pallas_call(
        load_kernel,
        in_specs=[ANY_SPEC] * len(arrays),
        out_specs=[VMEM_SPEC] * len(arrays),
        out_shape=[pltpu.VMEM(array.shape, array.dtype) for array in arrays],
        scratch_shapes=[pltpu.SemaphoreType.DMA((len(arrays),))],
        compiler_params=pltpu.CompilerParams(vmem_limit_bytes=2**20),
        cost_estimate=pl.CostEstimate(
            flops=0, bytes_accessed=2 * sum(array.size * array.dtype.itemsize for array in arrays), transcendentals=0
        ),
    )(*map(in_hbm, arrays))


def forward_kernel(
    tokens_ref, encoder_ref, mate_encoder_ref, bias_ref, mate_bias_ref, decoder_ref, mate_decoder_ref, keep_ref, send_ref
):
    tokens = tokens_ref[...]

    def act(weight_ref, row_ref):
        pre = nt_dot(tokens, weight_ref[...]) + row_ref[...]
        return (softplus(sharpness * pre) / sharpness).astype(bf16)

    own = act(encoder_ref, bias_ref)
    mate = act(mate_encoder_ref, mate_bias_ref)
    half = keep_ref.shape[0]
    width = 1024
    for start in range(0, keep_ref.shape[1], width):
        columns = pl.ds(start, width)
        part = jnp.dot(own, decoder_ref[:, columns], preferred_element_type=f32) + jnp.dot(
            mate, mate_decoder_ref[:, columns], preferred_element_type=f32
        )
        keep_ref[:, columns] = part[:half]
        send_ref[:, columns] = part[half:].astype(bf16)


def forward(tokens, encoder, mate_encoder, bias, mate_bias, decoder, mate_decoder):
    half, features = tokens.shape[0] // 2, tokens.shape[1]
    latents = encoder.shape[0]
    return pl.pallas_call(
        forward_kernel,
        in_specs=[VMEM_SPEC] * 7,
        out_specs=[VMEM_SPEC] * 2,
        out_shape=[pltpu.VMEM((half, features), f32), pltpu.VMEM((half, features), bf16)],
        compiler_params=pltpu.CompilerParams(vmem_limit_bytes=16 * 2**20),
        cost_estimate=pl.CostEstimate(
            flops=16 * half * latents * features, bytes_accessed=8 * latents * features, transcendentals=8 * half * latents
        ),
    )(*map(in_vmem, (tokens, encoder, mate_encoder, bias, mate_bias, decoder, mate_decoder)))


def prepare_kernel(
    tokens_ref,
    mate_tokens_ref,
    encoder_ref,
    bias_ref,
    decoder_ref,
    encoder_first_ref,
    encoder_second_ref,
    decoder_first_ref,
    decoder_second_ref,
    gathered_ref,
    slope_ref,
    act_ref,
    floor_ref,
    pull_ref,
    encoder_first_out,
    encoder_second_out,
    decoder_first_out,
    decoder_second_out,
    sems,
):
    moves = [
        (encoder_first_ref, encoder_first_out),
        (encoder_second_ref, encoder_second_out),
        (decoder_first_ref, decoder_first_out),
        (decoder_second_ref, decoder_second_out),
    ]
    pieces = sems.shape[1]
    width = encoder_first_ref.shape[1] // pieces
    copies = [
        pltpu.make_async_copy(
            source.at[:, pl.ds(piece * width, width)], target.at[:, pl.ds(piece * width, width)], sems.at[which, piece]
        )
        for which, (source, target) in enumerate(moves)
        for piece in range(pieces)
    ]
    for copy in copies:
        copy.start()
    tokens = jnp.concatenate([tokens_ref[...], mate_tokens_ref[...]], axis=0)
    gathered_ref[...] = tokens
    pre = nt_dot(encoder_ref[...], tokens) + turn(bias_ref[...])
    act = softplus(sharpness * pre) / sharpness
    slope_ref[...] = jax.nn.sigmoid(sharpness * pre)
    act_ref[...] = act.astype(bf16)
    decoder = decoder_ref[...].astype(f32)
    norms = jnp.sqrt(jnp.sum(decoder * decoder, axis=1, keepdims=True) + 1e-06)
    floor_ref[...] = sparsity_coef * norms
    pull_ref[...] = sparsity_coef * jnp.sum(act, axis=1, keepdims=True) / norms
    for copy in copies:
        copy.wait()


def prepare(tokens, mate_tokens, encoder, bias, decoder, *moments):
    latents, features = encoder.shape
    count = 2 * tokens.shape[0]
    return pl.pallas_call(
        prepare_kernel,
        in_specs=[VMEM_SPEC] * 5 + [ANY_SPEC] * 4,
        out_specs=[VMEM_SPEC] * 9,
        out_shape=[
            pltpu.VMEM((count, features), bf16),
            pltpu.VMEM((latents, count), f32),
            pltpu.VMEM((latents, count), bf16),
            pltpu.VMEM((latents, 1), f32),
            pltpu.VMEM((latents, 1), f32),
        ]
        + [pltpu.VMEM((latents, features), f32)] * 4,
        scratch_shapes=[pltpu.SemaphoreType.DMA((4, 2))],
        compiler_params=pltpu.CompilerParams(vmem_limit_bytes=16 * 2**20),
        cost_estimate=pl.CostEstimate(
            flops=2 * count * latents * features, bytes_accessed=20 * latents * features, transcendentals=3 * count * latents
        ),
    )(*map(in_vmem, (tokens, mate_tokens, encoder, bias, decoder)), *map(in_hbm, moments))


DECODER_BLOCKS = (1,) * 8
ENCODER_BLOCKS = (1,) * 8


def update_kernel(
    own,
    errors_ref,
    tokens_ref,
    slope_ref,
    act_ref,
    floor_ref,
    pull_ref,
    encoder_first_ref,
    encoder_second_ref,
    decoder_first_ref,
    decoder_second_ref,
    encoder_ref,
    decoder_ref,
    encoder_bias_ref,
    latent_first_ref,
    latent_second_ref,
    decoder_bias_ref,
    feature_first_ref,
    feature_second_ref,
    *refs,
):
    outs, slots, (pre_ref, sems) = refs[:12], refs[12:24], refs[24:]
    features = encoder_ref.shape[1]

    def send(which, columns=slice(None)):
        pltpu.make_async_copy(slots[which].at[:, columns], outs[which].at[:, columns], sems.at[which]).start()

    def blocks(eighths):
        start = 0
        for count in eighths:
            width = features // 8 * count
            yield pl.ds(start, width)
            start += width

    for columns in blocks(DECODER_BLOCKS):
        weight = decoder_ref[:, columns].astype(f32)
        grad = jnp.dot(act_ref[...], errors_ref[:, columns], preferred_element_type=f32) + pull_ref[...] * weight
        new, slots[4][:, columns], slots[5][:, columns] = adam_update(
            weight, grad, decoder_first_ref[:, columns], decoder_second_ref[:, columns]
        )
        slots[1][:, columns] = new.astype(bf16)
        for which in (1, 4, 5):
            send(which, columns)

    grad = (nt_dot(decoder_ref[...], errors_ref[...]) + floor_ref[...]) * slope_ref[...]
    pre_ref[...] = grad.astype(bf16)
    total = turn(jnp.sum(grad, axis=1, keepdims=True))
    slots[6][...], slots[7][...], slots[8][...] = adam_update(
        encoder_bias_ref[...], total, latent_first_ref[...], latent_second_ref[...]
    )
    for which in range(6, 9):
        send(which)

    for columns in blocks(ENCODER_BLOCKS):
        grad = jnp.dot(pre_ref[...], tokens_ref[:, columns], preferred_element_type=f32)
        new, slots[2][:, columns], slots[3][:, columns] = adam_update(
            encoder_ref[:, columns], grad, encoder_first_ref[:, columns], encoder_second_ref[:, columns]
        )
        slots[0][:, columns] = new.astype(bf16)
        for which in (0, 2, 3):
            send(which, columns)
    rows = errors_ref[...].astype(f32)
    while rows.shape[0] > own:
        half = rows.shape[0] // 2
        rows = rows[:half] + rows[half:]
    total = rows[0:1]
    for row in range(1, own):
        total = total + rows[row : row + 1]
    slots[9][...], slots[10][...], slots[11][...] = adam_update(
        decoder_bias_ref[...], total, feature_first_ref[...], feature_second_ref[...]
    )
    for which in range(9, 12):
        send(which)
    for which in range(12):
        pltpu.make_async_copy(slots[which], outs[which], sems.at[which]).wait()


def update(own, errors, prepared, encoder, decoder, *short):
    latents, features = encoder.shape
    count = errors.shape[0]
    shapes = [((latents, features), bf16)] * 2 + [((latents, features), f32)] * 4
    shapes += [((1, latents), f32)] * 3 + [((1, features), f32)] * 3
    return pl.pallas_call(
        functools.partial(update_kernel, own),
        in_specs=[VMEM_SPEC] * 18,
        out_specs=[ANY_SPEC] * 12,
        out_shape=[jax.ShapeDtypeStruct(*shape) for shape in shapes],
        scratch_shapes=[pltpu.VMEM(*shape) for shape in shapes]
        + [pltpu.VMEM((latents, count), bf16), pltpu.SemaphoreType.DMA((12,))],
        compiler_params=pltpu.CompilerParams(vmem_limit_bytes=24 * 2**20),
        cost_estimate=pl.CostEstimate(
            flops=6 * count * latents * features,
            bytes_accessed=40 * latents * features,
            transcendentals=4 * latents * features,
        ),
    )(*map(in_vmem, (errors, *prepared, encoder, decoder, *short)))


def local(
    devices,
    tokens,
    encoder_weight,
    encoder_bias,
    decoder_weight,
    decoder_bias,
    encoder_first,
    encoder_second,
    decoder_first,
    decoder_second,
    latent_first,
    latent_second,
    feature_first,
    feature_second,
):
    bits = [1 << b for b in reversed(range(1, devices.bit_length() - 1))]
    own = tokens.shape[0]
    row = lambda array: array.reshape(1, -1)
    encoder_bias, latent_first, latent_second, decoder_bias, feature_first, feature_second = map(
        row, (encoder_bias, latent_first, latent_second, decoder_bias, feature_first, feature_second)
    )
    far = swap(tokens, bits[0], devices)
    column, encoder, decoder, bias = load(tokens, encoder_weight, decoder_weight, encoder_bias)
    column = lax.optimization_barrier(jnp.concatenate([column, far], axis=0))
    mate_encoder = swap(encoder, 1, devices)
    mate_bias = swap(bias, 1, devices)
    mate_decoder = swap(decoder, 1, devices)
    for bit in bits[1:]:
        column = lax.optimization_barrier(jnp.concatenate([column, swap(column, bit, devices)], axis=0))
    part, send = forward(column, encoder, mate_encoder, bias, mate_bias, decoder, mate_decoder)
    part = part + swap(send, bits[-1], devices).astype(f32)
    mate_column = swap(column, 1, devices)
    half = part.shape[0]
    for level in reversed(range(len(bits) - 1)):
        part = lax.reduce_precision(part, 8, 7)
        sent = part.astype(bf16)
        if level == 0:
            sent, mate_column = lax.optimization_barrier((sent, mate_column))
        other = swap(sent, bits[level], devices)
        if level == 0:
            prepared = prepare(
                column, mate_column, encoder, bias, decoder, encoder_first, encoder_second, decoder_first, decoder_second
            )
            other, prepared = lax.optimization_barrier((other, prepared))
        size = own << level
        pieces = [other[start ^ size : (start ^ size) + size] for start in range(0, half, size)]
        part = part + jnp.concatenate(pieces, axis=0).astype(f32)
    errors = (part + decoder_bias - column[:half].astype(f32)).astype(bf16)
    errors = lax.optimization_barrier(jnp.concatenate([errors, swap(errors, bits[-1], devices)], axis=0))
    errors = jnp.concatenate([errors, swap(errors, 1, devices)], axis=0)
    out = update(
        own,
        errors,
        prepared,
        encoder,
        decoder,
        bias,
        latent_first,
        latent_second,
        decoder_bias,
        feature_first,
        feature_second,
    )
    new_encoder, new_decoder, enc_first, enc_second, dec_first, dec_second = out[:6]
    lat_new, lat_first, lat_second, feat_new, feat_first, feat_second = (array.reshape(-1) for array in out[6:])
    return (
        new_encoder,
        lat_new,
        new_decoder,
        feat_new,
        enc_first,
        enc_second,
        dec_first,
        dec_second,
        lat_first,
        lat_second,
        feat_first,
        feat_second,
    )


def solution(mesh):
    devices = mesh.shape["dict"]
    in_specs = (
        P(("groups", "dict"), None),
        P(("groups", "dict"), None),
        P(("groups", "dict")),
        P(("groups", "dict"), None),
        P("groups"),
        P(("groups", "dict"), None),
        P(("groups", "dict"), None),
        P(("groups", "dict"), None),
        P(("groups", "dict"), None),
        P(("groups", "dict")),
        P(("groups", "dict")),
        P("groups"),
        P("groups"),
    )
    out_specs = (
        P(("groups", "dict"), None),
        P(("groups", "dict")),
        P(("groups", "dict"), None),
        P("groups"),
        P(("groups", "dict"), None),
        P(("groups", "dict"), None),
        P(("groups", "dict"), None),
        P(("groups", "dict"), None),
        P(("groups", "dict")),
        P(("groups", "dict")),
        P("groups"),
        P("groups"),
    )

    def step(*args):
        return local(devices, *args)

    return jax.shard_map(step, mesh=mesh, in_specs=in_specs, out_specs=out_specs, check_vma=False)
```

```python
import functools

import jax
import jax.numpy as jnp
from jax import lax
from jax.experimental import pallas as pl
from jax.experimental.pallas import tpu as pltpu
from jax.sharding import PartitionSpec as P

STEP = 100


sharpness = 4.0
sparsity_coef = 0.3
first_decay = 0.9
second_decay = 0.999
learn_rate = 0.001
epsilon = 1e-08

f32 = jnp.float32
bf16 = jnp.bfloat16


def adam_update(param, grad, first, second):
    first_new = first_decay * first + (1.0 - first_decay) * grad
    second_new = second_decay * second + (1.0 - second_decay) * grad * grad
    first_corr = 1.0 - first_decay**STEP
    second_corr = 1.0 - second_decay**STEP
    square = second_new * (1.0 / second_corr)
    root = square * lax.rsqrt(square)
    change = (learn_rate / first_corr) * first_new / (root + epsilon)
    return (param.astype(f32) - change, first_new, second_new)


def softplus(x):
    return jnp.maximum(x, 0.0) + jnp.log1p(jnp.exp(-jnp.abs(x)))


def nt_dot(a, b):
    return lax.dot_general(a, b, (((1,), (1,)), ((), ())), preferred_element_type=f32)


def turn(vector):
    side = max(vector.shape)
    square = (side, side)
    diagonal = lax.broadcasted_iota(jnp.int32, square, 0) == lax.broadcasted_iota(jnp.int32, square, 1)
    axis = 1 if vector.shape[0] == 1 else 0
    return jnp.sum(jnp.where(diagonal, jnp.broadcast_to(vector, square), 0.0), axis=axis, keepdims=True)


def swap(x, bit, devices):
    return lax.ppermute(x, "dict", [(i, i ^ bit) for i in range(devices)])


def in_vmem(array):
    return pltpu.with_memory_space_constraint(array, pltpu.VMEM)


def in_hbm(array):
    return pltpu.with_memory_space_constraint(array, pltpu.HBM)


VMEM_SPEC = pl.BlockSpec(memory_space=pltpu.VMEM)
ANY_SPEC = pl.BlockSpec(memory_space=pl.ANY)


def load_kernel(*refs):
    count = len(refs) // 2
    copies = [pltpu.make_async_copy(refs[i], refs[count + i], refs[-1].at[i]) for i in range(count)]
    for copy in copies:
        copy.start()
    for copy in copies:
        copy.wait()


def load(*arrays):
    return pl.pallas_call(
        load_kernel,
        in_specs=[ANY_SPEC] * len(arrays),
        out_specs=[VMEM_SPEC] * len(arrays),
        out_shape=[pltpu.VMEM(array.shape, array.dtype) for array in arrays],
        scratch_shapes=[pltpu.SemaphoreType.DMA((len(arrays),))],
        compiler_params=pltpu.CompilerParams(vmem_limit_bytes=2**20),
        cost_estimate=pl.CostEstimate(
            flops=0, bytes_accessed=2 * sum(array.size * array.dtype.itemsize for array in arrays), transcendentals=0
        ),
    )(*map(in_hbm, arrays))


def forward_kernel(
    tokens_ref,
    encoder_ref,
    mate_encoder_ref,
    bias_ref,
    mate_bias_ref,
    decoder_ref,
    mate_decoder_ref,
    keep_ref,
    *send_refs,
):
    tokens = tokens_ref[...]

    def act(weight_ref, row_ref):
        pre = nt_dot(tokens, weight_ref[...]) + row_ref[...]
        return (softplus(sharpness * pre) / sharpness).astype(bf16)

    own = act(encoder_ref, bias_ref)
    mate = act(mate_encoder_ref, mate_bias_ref)
    rows = keep_ref.shape[0]
    width = 1024
    for start in range(0, keep_ref.shape[1], width):
        columns = pl.ds(start, width)
        part = jnp.dot(own, decoder_ref[:, columns], preferred_element_type=f32) + jnp.dot(
            mate, mate_decoder_ref[:, columns], preferred_element_type=f32
        )
        keep_ref[:, columns] = part[:rows]
        for quarter, send_ref in enumerate(send_refs, 1):
            send_ref[:, columns] = part[quarter * rows : (quarter + 1) * rows].astype(bf16)


def forward(tokens, encoder, mate_encoder, bias, mate_bias, decoder, mate_decoder):
    rows, features = tokens.shape[0] // 4, tokens.shape[1]
    latents = encoder.shape[0]
    return pl.pallas_call(
        forward_kernel,
        in_specs=[VMEM_SPEC] * 7,
        out_specs=[VMEM_SPEC] * 4,
        out_shape=[pltpu.VMEM((rows, features), f32)] + [pltpu.VMEM((rows, features), bf16)] * 3,
        compiler_params=pltpu.CompilerParams(vmem_limit_bytes=16 * 2**20),
        cost_estimate=pl.CostEstimate(
            flops=32 * rows * latents * features, bytes_accessed=8 * latents * features, transcendentals=16 * rows * latents
        ),
    )(*map(in_vmem, (tokens, encoder, mate_encoder, bias, mate_bias, decoder, mate_decoder)))


def prepare_kernel(
    tokens_ref, mate_tokens_ref, encoder_ref, bias_ref, decoder_ref, gathered_ref, slope_ref, act_ref, floor_ref, pull_ref
):
    tokens = jnp.concatenate([tokens_ref[...], mate_tokens_ref[...]], axis=0)
    gathered_ref[...] = tokens
    pre = nt_dot(encoder_ref[...], tokens) + turn(bias_ref[...])
    act = softplus(sharpness * pre) / sharpness
    slope_ref[...] = jax.nn.sigmoid(sharpness * pre)
    act_ref[...] = act.astype(bf16)
    decoder = decoder_ref[...].astype(f32)
    norms = jnp.sqrt(jnp.sum(decoder * decoder, axis=1, keepdims=True) + 1e-06)
    floor_ref[...] = sparsity_coef * norms
    pull_ref[...] = sparsity_coef * jnp.sum(act, axis=1, keepdims=True) / norms


def prepare(tokens, mate_tokens, encoder, bias, decoder):
    latents, features = encoder.shape
    count = 2 * tokens.shape[0]
    return pl.pallas_call(
        prepare_kernel,
        in_specs=[VMEM_SPEC] * 5,
        out_specs=[VMEM_SPEC] * 5,
        out_shape=[
            pltpu.VMEM((count, features), bf16),
            pltpu.VMEM((latents, count), f32),
            pltpu.VMEM((latents, count), bf16),
            pltpu.VMEM((latents, 1), f32),
            pltpu.VMEM((latents, 1), f32),
        ],
        compiler_params=pltpu.CompilerParams(vmem_limit_bytes=16 * 2**20),
        cost_estimate=pl.CostEstimate(
            flops=2 * count * latents * features, bytes_accessed=10 * latents * features, transcendentals=3 * count * latents
        ),
    )(*map(in_vmem, (tokens, mate_tokens, encoder, bias, decoder)))


DECODER_BLOCKS = (1,) * 8
ENCODER_BLOCKS = (1,) * 8


def update_kernel(
    own,
    errors_ref,
    tokens_ref,
    slope_ref,
    act_ref,
    floor_ref,
    pull_ref,
    encoder_first_ref,
    encoder_second_ref,
    decoder_first_ref,
    decoder_second_ref,
    encoder_ref,
    decoder_ref,
    encoder_bias_ref,
    latent_first_ref,
    latent_second_ref,
    decoder_bias_ref,
    feature_first_ref,
    feature_second_ref,
    *refs,
):
    outs, slots, (pre_ref, sems) = refs[:12], refs[12:24], refs[24:]
    features = encoder_ref.shape[1]

    def send(which, columns=slice(None)):
        pltpu.make_async_copy(slots[which].at[:, columns], outs[which].at[:, columns], sems.at[which]).start()

    def blocks(eighths):
        start = 0
        for count in eighths:
            width = features // 8 * count
            yield pl.ds(start, width)
            start += width

    for columns in blocks(DECODER_BLOCKS):
        weight = decoder_ref[:, columns].astype(f32)
        grad = jnp.dot(act_ref[...], errors_ref[:, columns], preferred_element_type=f32) + pull_ref[...] * weight
        new, slots[4][:, columns], slots[5][:, columns] = adam_update(
            weight, grad, decoder_first_ref[:, columns], decoder_second_ref[:, columns]
        )
        slots[1][:, columns] = new.astype(bf16)
        for which in (1, 4, 5):
            send(which, columns)

    grad = (nt_dot(decoder_ref[...], errors_ref[...]) + floor_ref[...]) * slope_ref[...]
    pre_ref[...] = grad.astype(bf16)
    total = turn(jnp.sum(grad, axis=1, keepdims=True))
    slots[6][...], slots[7][...], slots[8][...] = adam_update(
        encoder_bias_ref[...], total, latent_first_ref[...], latent_second_ref[...]
    )
    for which in range(6, 9):
        send(which)

    for columns in blocks(ENCODER_BLOCKS):
        grad = jnp.dot(pre_ref[...], tokens_ref[:, columns], preferred_element_type=f32)
        new, slots[2][:, columns], slots[3][:, columns] = adam_update(
            encoder_ref[:, columns], grad, encoder_first_ref[:, columns], encoder_second_ref[:, columns]
        )
        slots[0][:, columns] = new.astype(bf16)
        for which in (0, 2, 3):
            send(which, columns)
    rows = errors_ref[...].astype(f32)
    while rows.shape[0] > own:
        half = rows.shape[0] // 2
        rows = rows[:half] + rows[half:]
    total = rows[0:1]
    for row in range(1, own):
        total = total + rows[row : row + 1]
    slots[9][...], slots[10][...], slots[11][...] = adam_update(
        decoder_bias_ref[...], total, feature_first_ref[...], feature_second_ref[...]
    )
    for which in range(9, 12):
        send(which)
    for which in range(12):
        pltpu.make_async_copy(slots[which], outs[which], sems.at[which]).wait()


def update(own, errors, prepared, encoder, decoder, *short):
    latents, features = encoder.shape
    count = errors.shape[0]
    shapes = [((latents, features), bf16)] * 2 + [((latents, features), f32)] * 4
    shapes += [((1, latents), f32)] * 3 + [((1, features), f32)] * 3
    return pl.pallas_call(
        functools.partial(update_kernel, own),
        in_specs=[VMEM_SPEC] * 18,
        out_specs=[ANY_SPEC] * 12,
        out_shape=[jax.ShapeDtypeStruct(*shape) for shape in shapes],
        scratch_shapes=[pltpu.VMEM(*shape) for shape in shapes]
        + [pltpu.VMEM((latents, count), bf16), pltpu.SemaphoreType.DMA((12,))],
        compiler_params=pltpu.CompilerParams(vmem_limit_bytes=24 * 2**20),
        cost_estimate=pl.CostEstimate(
            flops=6 * count * latents * features,
            bytes_accessed=40 * latents * features,
            transcendentals=4 * latents * features,
        ),
    )(*map(in_vmem, (errors, *prepared, encoder, decoder, *short)))


def local(
    devices,
    tokens,
    encoder_weight,
    encoder_bias,
    decoder_weight,
    decoder_bias,
    encoder_first,
    encoder_second,
    decoder_first,
    decoder_second,
    latent_first,
    latent_second,
    feature_first,
    feature_second,
):
    far = [1 << b for b in reversed(range(3, devices.bit_length() - 1))]
    near = (4, 2, 6)
    own = tokens.shape[0]
    row = lambda array: array.reshape(1, -1)
    encoder_bias, latent_first, latent_second, decoder_bias, feature_first, feature_second = map(
        row, (encoder_bias, latent_first, latent_second, decoder_bias, feature_first, feature_second)
    )
    other = swap(tokens, far[0], devices)
    (column,) = load(tokens)
    mate_encoder = swap(encoder_weight, 1, devices)
    mate_decoder = swap(decoder_weight, 1, devices)
    mate_bias = swap(encoder_bias, 1, devices)
    encoder, decoder, bias = load(encoder_weight, decoder_weight, encoder_bias)
    column = lax.optimization_barrier(jnp.concatenate([column, other], axis=0))
    for bit in far[1:]:
        column = lax.optimization_barrier(jnp.concatenate([column, swap(column, bit, devices)], axis=0))
    rows = column.shape[0]
    column = lax.optimization_barrier(jnp.concatenate([column] + [swap(column, bits, devices) for bits in near], axis=0))
    part, *sent = forward(column, encoder, mate_encoder, bias, mate_bias, decoder, mate_decoder)
    received = {bits: swap(piece, bits, devices) for bits, piece in reversed(list(zip(near, sent)))}
    moments = load(encoder_first, encoder_second, decoder_first, decoder_second)
    received, moments = lax.optimization_barrier((received, moments))
    for bits in (6, 4, 2):
        part = part + received[bits].astype(f32)
    for level in reversed(range(len(far))):
        part = lax.reduce_precision(part, 8, 7)
        piece = part.astype(bf16)
        other = swap(piece, far[level], devices)
        size = own << level
        pieces = [other[start ^ size : (start ^ size) + size] for start in range(0, rows, size)]
        part = part + jnp.concatenate(pieces, axis=0).astype(f32)
    errors = (part + decoder_bias - column[:rows].astype(f32)).astype(bf16)
    errors, column = lax.optimization_barrier((errors, column))
    received = [swap(errors, bits, devices) for bits in near]
    prepared = prepare(column, swap(column, 1, devices), encoder, bias, decoder)
    errors = lax.optimization_barrier(jnp.concatenate([errors] + received, axis=0))
    errors = jnp.concatenate([errors, swap(errors, 1, devices)], axis=0)
    out = update(
        own,
        errors,
        (*prepared, *moments),
        encoder,
        decoder,
        bias,
        latent_first,
        latent_second,
        decoder_bias,
        feature_first,
        feature_second,
    )
    new_encoder, new_decoder, enc_first, enc_second, dec_first, dec_second = out[:6]
    lat_new, lat_first, lat_second, feat_new, feat_first, feat_second = (array.reshape(-1) for array in out[6:])
    return (
        new_encoder,
        lat_new,
        new_decoder,
        feat_new,
        enc_first,
        enc_second,
        dec_first,
        dec_second,
        lat_first,
        lat_second,
        feat_first,
        feat_second,
    )


def solution(mesh):
    devices = mesh.shape["dict"]
    in_specs = (
        P(("groups", "dict"), None),
        P(("groups", "dict"), None),
        P(("groups", "dict")),
        P(("groups", "dict"), None),
        P("groups"),
        P(("groups", "dict"), None),
        P(("groups", "dict"), None),
        P(("groups", "dict"), None),
        P(("groups", "dict"), None),
        P(("groups", "dict")),
        P(("groups", "dict")),
        P("groups"),
        P("groups"),
    )
    out_specs = (
        P(("groups", "dict"), None),
        P(("groups", "dict")),
        P(("groups", "dict"), None),
        P("groups"),
        P(("groups", "dict"), None),
        P(("groups", "dict"), None),
        P(("groups", "dict"), None),
        P(("groups", "dict"), None),
        P(("groups", "dict")),
        P(("groups", "dict")),
        P("groups"),
        P("groups"),
    )

    def step(*args):
        return local(devices, *args)

    return jax.shard_map(step, mesh=mesh, in_specs=in_specs, out_specs=out_specs, check_vma=False)
```

```python
import functools

import jax
import jax.numpy as jnp
from jax import lax
from jax.experimental import pallas as pl
from jax.experimental.pallas import tpu as pltpu
from jax.sharding import PartitionSpec as P

STEP = 100


sharpness = 4.0
sparsity_coef = 0.3
first_decay = 0.9
second_decay = 0.999
learn_rate = 0.001
epsilon = 1e-08

f32 = jnp.float32
bf16 = jnp.bfloat16


def adam_update(param, grad, first, second):
    first_new = first_decay * first + (1.0 - first_decay) * grad
    second_new = second_decay * second + (1.0 - second_decay) * grad * grad
    first_corr = 1.0 - first_decay**STEP
    second_corr = 1.0 - second_decay**STEP
    square = second_new * (1.0 / second_corr)
    root = square * lax.rsqrt(square)
    change = (learn_rate / first_corr) * first_new / (root + epsilon)
    return (param.astype(f32) - change, first_new, second_new)


def softplus(x):
    return jnp.maximum(x, 0.0) + jnp.log1p(jnp.exp(-jnp.abs(x)))


def nt_dot(a, b):
    return lax.dot_general(a, b, (((1,), (1,)), ((), ())), preferred_element_type=f32)


def turn(vector):
    side = max(vector.shape)
    square = (side, side)
    diagonal = lax.broadcasted_iota(jnp.int32, square, 0) == lax.broadcasted_iota(jnp.int32, square, 1)
    axis = 1 if vector.shape[0] == 1 else 0
    return jnp.sum(jnp.where(diagonal, jnp.broadcast_to(vector, square), 0.0), axis=axis, keepdims=True)


def swap(x, bit, devices):
    return lax.ppermute(x, "dict", [(i, i ^ bit) for i in range(devices)])


def in_vmem(array):
    return pltpu.with_memory_space_constraint(array, pltpu.VMEM)


def in_hbm(array):
    return pltpu.with_memory_space_constraint(array, pltpu.HBM)


VMEM_SPEC = pl.BlockSpec(memory_space=pltpu.VMEM)
ANY_SPEC = pl.BlockSpec(memory_space=pl.ANY)


def load_kernel(*refs):
    count = len(refs) // 2
    copies = [pltpu.make_async_copy(refs[i], refs[count + i], refs[-1].at[i]) for i in range(count)]
    for copy in copies:
        copy.start()
    for copy in copies:
        copy.wait()


def load(*arrays):
    return pl.pallas_call(
        load_kernel,
        in_specs=[ANY_SPEC] * len(arrays),
        out_specs=[VMEM_SPEC] * len(arrays),
        out_shape=[pltpu.VMEM(array.shape, array.dtype) for array in arrays],
        scratch_shapes=[pltpu.SemaphoreType.DMA((len(arrays),))],
        compiler_params=pltpu.CompilerParams(vmem_limit_bytes=2**20),
        cost_estimate=pl.CostEstimate(
            flops=0, bytes_accessed=2 * sum(array.size * array.dtype.itemsize for array in arrays), transcendentals=0
        ),
    )(*map(in_hbm, arrays))


def forward_kernel(
    tokens_ref,
    encoder_ref,
    mate_encoder_ref,
    bias_ref,
    mate_bias_ref,
    decoder_ref,
    mate_decoder_ref,
    keep_ref,
    *send_refs,
):
    tokens = tokens_ref[...]

    def act(weight_ref, row_ref):
        pre = nt_dot(tokens, weight_ref[...]) + row_ref[...]
        return (softplus(sharpness * pre) / sharpness).astype(bf16)

    own = act(encoder_ref, bias_ref)
    mate = act(mate_encoder_ref, mate_bias_ref)
    rows = keep_ref.shape[0]
    width = 1024
    for start in range(0, keep_ref.shape[1], width):
        columns = pl.ds(start, width)
        part = jnp.dot(own, decoder_ref[:, columns], preferred_element_type=f32) + jnp.dot(
            mate, mate_decoder_ref[:, columns], preferred_element_type=f32
        )
        keep_ref[:, columns] = part[:rows]
        for quarter, send_ref in enumerate(send_refs, 1):
            send_ref[:, columns] = part[quarter * rows : (quarter + 1) * rows].astype(bf16)


def forward(tokens, encoder, mate_encoder, bias, mate_bias, decoder, mate_decoder):
    rows, features = tokens.shape[0] // 4, tokens.shape[1]
    latents = encoder.shape[0]
    return pl.pallas_call(
        forward_kernel,
        in_specs=[VMEM_SPEC] * 7,
        out_specs=[VMEM_SPEC] * 4,
        out_shape=[pltpu.VMEM((rows, features), f32)] + [pltpu.VMEM((rows, features), bf16)] * 3,
        compiler_params=pltpu.CompilerParams(vmem_limit_bytes=16 * 2**20),
        cost_estimate=pl.CostEstimate(
            flops=32 * rows * latents * features, bytes_accessed=8 * latents * features, transcendentals=16 * rows * latents
        ),
    )(*map(in_vmem, (tokens, encoder, mate_encoder, bias, mate_bias, decoder, mate_decoder)))


def prepare_kernel(
    tokens_ref, mate_tokens_ref, encoder_ref, bias_ref, decoder_ref, gathered_ref, slope_ref, act_ref, floor_ref, pull_ref
):
    tokens = jnp.concatenate([tokens_ref[...], mate_tokens_ref[...]], axis=0)
    gathered_ref[...] = tokens
    pre = nt_dot(encoder_ref[...], tokens) + turn(bias_ref[...])
    act = softplus(sharpness * pre) / sharpness
    slope_ref[...] = jax.nn.sigmoid(sharpness * pre)
    act_ref[...] = act.astype(bf16)
    decoder = decoder_ref[...].astype(f32)
    norms = jnp.sqrt(jnp.sum(decoder * decoder, axis=1, keepdims=True) + 1e-06)
    floor_ref[...] = sparsity_coef * norms
    pull_ref[...] = sparsity_coef * jnp.sum(act, axis=1, keepdims=True) / norms


def prepare(tokens, mate_tokens, encoder, bias, decoder):
    latents, features = encoder.shape
    count = 2 * tokens.shape[0]
    return pl.pallas_call(
        prepare_kernel,
        in_specs=[VMEM_SPEC] * 5,
        out_specs=[VMEM_SPEC] * 5,
        out_shape=[
            pltpu.VMEM((count, features), bf16),
            pltpu.VMEM((latents, count), f32),
            pltpu.VMEM((latents, count), bf16),
            pltpu.VMEM((latents, 1), f32),
            pltpu.VMEM((latents, 1), f32),
        ],
        compiler_params=pltpu.CompilerParams(vmem_limit_bytes=16 * 2**20),
        cost_estimate=pl.CostEstimate(
            flops=2 * count * latents * features, bytes_accessed=10 * latents * features, transcendentals=3 * count * latents
        ),
    )(*map(in_vmem, (tokens, mate_tokens, encoder, bias, decoder)))


DECODER_BLOCKS = (1,) * 8
ENCODER_BLOCKS = (1,) * 8


def update_kernel(
    own,
    errors_ref,
    tokens_ref,
    slope_ref,
    act_ref,
    floor_ref,
    pull_ref,
    encoder_first_ref,
    encoder_second_ref,
    decoder_first_ref,
    decoder_second_ref,
    encoder_ref,
    decoder_ref,
    encoder_bias_ref,
    latent_first_ref,
    latent_second_ref,
    decoder_bias_ref,
    feature_first_ref,
    feature_second_ref,
    *refs,
):
    outs, slots, (pre_ref, sems) = refs[:12], refs[12:24], refs[24:]
    features = encoder_ref.shape[1]

    def send(which, columns=slice(None)):
        pltpu.make_async_copy(slots[which].at[:, columns], outs[which].at[:, columns], sems.at[which]).start()

    def blocks(eighths):
        start = 0
        for count in eighths:
            width = features // 8 * count
            yield pl.ds(start, width)
            start += width

    for columns in blocks(DECODER_BLOCKS):
        weight = decoder_ref[:, columns].astype(f32)
        grad = jnp.dot(act_ref[...], errors_ref[:, columns], preferred_element_type=f32) + pull_ref[...] * weight
        new, slots[4][:, columns], slots[5][:, columns] = adam_update(
            weight, grad, decoder_first_ref[:, columns], decoder_second_ref[:, columns]
        )
        slots[1][:, columns] = new.astype(bf16)
        for which in (1, 4, 5):
            send(which, columns)

    grad = (nt_dot(decoder_ref[...], errors_ref[...]) + floor_ref[...]) * slope_ref[...]
    pre_ref[...] = grad.astype(bf16)
    total = turn(jnp.sum(grad, axis=1, keepdims=True))
    slots[6][...], slots[7][...], slots[8][...] = adam_update(
        encoder_bias_ref[...], total, latent_first_ref[...], latent_second_ref[...]
    )
    for which in range(6, 9):
        send(which)

    for columns in blocks(ENCODER_BLOCKS):
        grad = jnp.dot(pre_ref[...], tokens_ref[:, columns], preferred_element_type=f32)
        new, slots[2][:, columns], slots[3][:, columns] = adam_update(
            encoder_ref[:, columns], grad, encoder_first_ref[:, columns], encoder_second_ref[:, columns]
        )
        slots[0][:, columns] = new.astype(bf16)
        for which in (0, 2, 3):
            send(which, columns)
    rows = errors_ref[...].astype(f32)
    while rows.shape[0] > own:
        half = rows.shape[0] // 2
        rows = rows[:half] + rows[half:]
    total = rows[0:1]
    for row in range(1, own):
        total = total + rows[row : row + 1]
    slots[9][...], slots[10][...], slots[11][...] = adam_update(
        decoder_bias_ref[...], total, feature_first_ref[...], feature_second_ref[...]
    )
    for which in range(9, 12):
        send(which)
    for which in range(12):
        pltpu.make_async_copy(slots[which], outs[which], sems.at[which]).wait()


def update(own, errors, prepared, encoder, decoder, *short):
    latents, features = encoder.shape
    count = errors.shape[0]
    shapes = [((latents, features), bf16)] * 2 + [((latents, features), f32)] * 4
    shapes += [((1, latents), f32)] * 3 + [((1, features), f32)] * 3
    return pl.pallas_call(
        functools.partial(update_kernel, own),
        in_specs=[VMEM_SPEC] * 18,
        out_specs=[ANY_SPEC] * 12,
        out_shape=[jax.ShapeDtypeStruct(*shape) for shape in shapes],
        scratch_shapes=[pltpu.VMEM(*shape) for shape in shapes]
        + [pltpu.VMEM((latents, count), bf16), pltpu.SemaphoreType.DMA((12,))],
        compiler_params=pltpu.CompilerParams(vmem_limit_bytes=24 * 2**20),
        cost_estimate=pl.CostEstimate(
            flops=6 * count * latents * features,
            bytes_accessed=40 * latents * features,
            transcendentals=4 * latents * features,
        ),
    )(*map(in_vmem, (errors, *prepared, encoder, decoder, *short)))


def local(
    devices,
    tokens,
    encoder_weight,
    encoder_bias,
    decoder_weight,
    decoder_bias,
    encoder_first,
    encoder_second,
    decoder_first,
    decoder_second,
    latent_first,
    latent_second,
    feature_first,
    feature_second,
):
    far = [1 << b for b in reversed(range(3, devices.bit_length() - 1))]
    near = (4, 2, 6)
    near_last = (2, 4, 6)
    near_sums = (2, 4, 6)
    own = tokens.shape[0]
    row = lambda array: array.reshape(1, -1)
    encoder_bias, latent_first, latent_second, decoder_bias, feature_first, feature_second = map(
        row, (encoder_bias, latent_first, latent_second, decoder_bias, feature_first, feature_second)
    )
    other = swap(tokens, far[0], devices)
    (column,) = load(tokens)
    mate_encoder = swap(encoder_weight, 1, devices)
    mate_decoder = swap(decoder_weight, 1, devices)
    mate_bias = swap(encoder_bias, 1, devices)
    encoder, decoder, bias = load(encoder_weight, decoder_weight, encoder_bias)
    column = lax.optimization_barrier(jnp.concatenate([column, other], axis=0))
    for bit in far[1:]:
        column = lax.optimization_barrier(jnp.concatenate([column, swap(column, bit, devices)], axis=0))
    rows = column.shape[0]
    blocks = {bits: swap(column, bits, devices) for bits in near}
    last_column = lax.optimization_barrier(jnp.concatenate([column] + [blocks[bits] for bits in near_last], axis=0))
    column = lax.optimization_barrier(jnp.concatenate([column] + [blocks[bits] for bits in near], axis=0))
    part, *sent = forward(column, encoder, mate_encoder, bias, mate_bias, decoder, mate_decoder)
    sent = dict(zip(near, sent))
    received = [swap(sent[bits], bits, devices) for bits in near_sums]
    moments = load(encoder_first, encoder_second, decoder_first, decoder_second)
    received, moments = lax.optimization_barrier((received, moments))
    for piece in received:
        part = part + piece.astype(f32)
    for level in reversed(range(len(far))):
        part = lax.reduce_precision(part, 8, 7)
        piece = part.astype(bf16)
        other = swap(piece, far[level], devices)
        size = own << level
        pieces = [other[start ^ size : (start ^ size) + size] for start in range(0, rows, size)]
        part = part + jnp.concatenate(pieces, axis=0).astype(f32)
    errors = (part + decoder_bias - column[:rows].astype(f32)).astype(bf16)
    column = last_column
    errors, column = lax.optimization_barrier((errors, column))
    received = [swap(errors, bits, devices) for bits in near_last]
    prepared = prepare(column, swap(column, 1, devices), encoder, bias, decoder)
    errors = lax.optimization_barrier(jnp.concatenate([errors] + received, axis=0))
    errors = jnp.concatenate([errors, swap(errors, 1, devices)], axis=0)
    out = update(
        own,
        errors,
        (*prepared, *moments),
        encoder,
        decoder,
        bias,
        latent_first,
        latent_second,
        decoder_bias,
        feature_first,
        feature_second,
    )
    new_encoder, new_decoder, enc_first, enc_second, dec_first, dec_second = out[:6]
    lat_new, lat_first, lat_second, feat_new, feat_first, feat_second = (array.reshape(-1) for array in out[6:])
    return (
        new_encoder,
        lat_new,
        new_decoder,
        feat_new,
        enc_first,
        enc_second,
        dec_first,
        dec_second,
        lat_first,
        lat_second,
        feat_first,
        feat_second,
    )


def solution(mesh):
    devices = mesh.shape["dict"]
    in_specs = (
        P(("groups", "dict"), None),
        P(("groups", "dict"), None),
        P(("groups", "dict")),
        P(("groups", "dict"), None),
        P("groups"),
        P(("groups", "dict"), None),
        P(("groups", "dict"), None),
        P(("groups", "dict"), None),
        P(("groups", "dict"), None),
        P(("groups", "dict")),
        P(("groups", "dict")),
        P("groups"),
        P("groups"),
    )
    out_specs = (
        P(("groups", "dict"), None),
        P(("groups", "dict")),
        P(("groups", "dict"), None),
        P("groups"),
        P(("groups", "dict"), None),
        P(("groups", "dict"), None),
        P(("groups", "dict"), None),
        P(("groups", "dict"), None),
        P(("groups", "dict")),
        P(("groups", "dict")),
        P("groups"),
        P("groups"),
    )

    def step(*args):
        return local(devices, *args)

    return jax.shard_map(step, mesh=mesh, in_specs=in_specs, out_specs=out_specs, check_vma=False)
```

```python
import functools

import jax
import jax.numpy as jnp
from jax import lax
from jax.experimental import pallas as pl
from jax.experimental.pallas import tpu as pltpu
from jax.sharding import PartitionSpec as P

STEP = 100


sharpness = 4.0
sparsity_coef = 0.3
first_decay = 0.9
second_decay = 0.999
learn_rate = 0.001
epsilon = 1e-08

f32 = jnp.float32
bf16 = jnp.bfloat16


def adam_update(param, grad, first, second):
    first_new = first_decay * first + (1.0 - first_decay) * grad
    second_new = second_decay * second + (1.0 - second_decay) * grad * grad
    first_corr = 1.0 - first_decay**STEP
    second_corr = 1.0 - second_decay**STEP
    square = second_new * (1.0 / second_corr)
    root = square * lax.rsqrt(square)
    change = (learn_rate / first_corr) * first_new / (root + epsilon)
    return (param.astype(f32) - change, first_new, second_new)


def softplus(x):
    return jnp.maximum(x, 0.0) + jnp.log1p(jnp.exp(-jnp.abs(x)))


def nt_dot(a, b):
    return lax.dot_general(a, b, (((1,), (1,)), ((), ())), preferred_element_type=f32)


def turn(vector):
    side = max(vector.shape)
    square = (side, side)
    diagonal = lax.broadcasted_iota(jnp.int32, square, 0) == lax.broadcasted_iota(jnp.int32, square, 1)
    axis = 1 if vector.shape[0] == 1 else 0
    return jnp.sum(jnp.where(diagonal, jnp.broadcast_to(vector, square), 0.0), axis=axis, keepdims=True)


def swap(x, bit, devices):
    return lax.ppermute(x, "dict", [(i, i ^ bit) for i in range(devices)])


def in_vmem(array):
    return pltpu.with_memory_space_constraint(array, pltpu.VMEM)


def in_hbm(array):
    return pltpu.with_memory_space_constraint(array, pltpu.HBM)


VMEM_SPEC = pl.BlockSpec(memory_space=pltpu.VMEM)
ANY_SPEC = pl.BlockSpec(memory_space=pl.ANY)


def load_kernel(*refs):
    count = len(refs) // 2
    copies = [pltpu.make_async_copy(refs[i], refs[count + i], refs[-1].at[i]) for i in range(count)]
    for copy in copies:
        copy.start()
    for copy in copies:
        copy.wait()


def load(*arrays):
    return pl.pallas_call(
        load_kernel,
        in_specs=[ANY_SPEC] * len(arrays),
        out_specs=[VMEM_SPEC] * len(arrays),
        out_shape=[pltpu.VMEM(array.shape, array.dtype) for array in arrays],
        scratch_shapes=[pltpu.SemaphoreType.DMA((len(arrays),))],
        compiler_params=pltpu.CompilerParams(vmem_limit_bytes=2**20),
        cost_estimate=pl.CostEstimate(
            flops=0, bytes_accessed=2 * sum(array.size * array.dtype.itemsize for array in arrays), transcendentals=0
        ),
    )(*map(in_hbm, arrays))


def forward_kernel(
    tokens_ref,
    encoder_ref,
    mate_encoder_ref,
    bias_ref,
    mate_bias_ref,
    decoder_ref,
    mate_decoder_ref,
    keep_ref,
    *send_refs,
):
    tokens = tokens_ref[...]

    def act(weight_ref, row_ref):
        pre = nt_dot(tokens, weight_ref[...]) + row_ref[...]
        return (softplus(sharpness * pre) / sharpness).astype(bf16)

    own = act(encoder_ref, bias_ref)
    mate = act(mate_encoder_ref, mate_bias_ref)
    rows = keep_ref.shape[0]
    width = 1024
    for start in range(0, keep_ref.shape[1], width):
        columns = pl.ds(start, width)
        part = jnp.dot(own, decoder_ref[:, columns], preferred_element_type=f32) + jnp.dot(
            mate, mate_decoder_ref[:, columns], preferred_element_type=f32
        )
        keep_ref[:, columns] = part[:rows]
        for quarter, send_ref in enumerate(send_refs, 1):
            send_ref[:, columns] = part[quarter * rows : (quarter + 1) * rows].astype(bf16)


def forward(tokens, encoder, mate_encoder, bias, mate_bias, decoder, mate_decoder):
    rows, features = tokens.shape[0] // 4, tokens.shape[1]
    latents = encoder.shape[0]
    return pl.pallas_call(
        forward_kernel,
        in_specs=[VMEM_SPEC] * 7,
        out_specs=[VMEM_SPEC] * 4,
        out_shape=[pltpu.VMEM((rows, features), f32)] + [pltpu.VMEM((rows, features), bf16)] * 3,
        compiler_params=pltpu.CompilerParams(vmem_limit_bytes=16 * 2**20),
        cost_estimate=pl.CostEstimate(
            flops=32 * rows * latents * features, bytes_accessed=8 * latents * features, transcendentals=16 * rows * latents
        ),
    )(*map(in_vmem, (tokens, encoder, mate_encoder, bias, mate_bias, decoder, mate_decoder)))


def prepare_kernel(
    tokens_ref, mate_tokens_ref, encoder_ref, bias_ref, decoder_ref, gathered_ref, slope_ref, act_ref, floor_ref, pull_ref
):
    tokens = jnp.concatenate([tokens_ref[...], mate_tokens_ref[...]], axis=0)
    gathered_ref[...] = tokens
    pre = nt_dot(encoder_ref[...], tokens) + turn(bias_ref[...])
    act = softplus(sharpness * pre) / sharpness
    slope_ref[...] = jax.nn.sigmoid(sharpness * pre)
    act_ref[...] = act.astype(bf16)
    decoder = decoder_ref[...].astype(f32)
    norms = jnp.sqrt(jnp.sum(decoder * decoder, axis=1, keepdims=True) + 1e-06)
    floor_ref[...] = sparsity_coef * norms
    pull_ref[...] = sparsity_coef * jnp.sum(act, axis=1, keepdims=True) / norms


def prepare(tokens, mate_tokens, encoder, bias, decoder):
    latents, features = encoder.shape
    count = 2 * tokens.shape[0]
    return pl.pallas_call(
        prepare_kernel,
        in_specs=[VMEM_SPEC] * 5,
        out_specs=[VMEM_SPEC] * 5,
        out_shape=[
            pltpu.VMEM((count, features), bf16),
            pltpu.VMEM((latents, count), f32),
            pltpu.VMEM((latents, count), bf16),
            pltpu.VMEM((latents, 1), f32),
            pltpu.VMEM((latents, 1), f32),
        ],
        compiler_params=pltpu.CompilerParams(vmem_limit_bytes=16 * 2**20),
        cost_estimate=pl.CostEstimate(
            flops=2 * count * latents * features, bytes_accessed=10 * latents * features, transcendentals=3 * count * latents
        ),
    )(*map(in_vmem, (tokens, mate_tokens, encoder, bias, decoder)))


DECODER_BLOCKS = (1,) * 8
ENCODER_BLOCKS = (1,) * 8


def update_kernel(
    own,
    errors_ref,
    tokens_ref,
    slope_ref,
    act_ref,
    floor_ref,
    pull_ref,
    encoder_first_ref,
    encoder_second_ref,
    decoder_first_ref,
    decoder_second_ref,
    encoder_ref,
    decoder_ref,
    encoder_bias_ref,
    latent_first_ref,
    latent_second_ref,
    decoder_bias_ref,
    feature_first_ref,
    feature_second_ref,
    *refs,
):
    outs, slots, (pre_ref, sems) = refs[:12], refs[12:24], refs[24:]
    features = encoder_ref.shape[1]

    def send(which, columns=slice(None)):
        pltpu.make_async_copy(slots[which].at[:, columns], outs[which].at[:, columns], sems.at[which]).start()

    def blocks(eighths):
        start = 0
        for count in eighths:
            width = features // 8 * count
            yield pl.ds(start, width)
            start += width

    act_grad = floor_ref[...]
    for columns in blocks(DECODER_BLOCKS):
        act_grad = act_grad + nt_dot(decoder_ref[:, columns], errors_ref[:, columns])
        weight = decoder_ref[:, columns].astype(f32)
        grad = jnp.dot(act_ref[...], errors_ref[:, columns], preferred_element_type=f32) + pull_ref[...] * weight
        new, slots[4][:, columns], slots[5][:, columns] = adam_update(
            weight, grad, decoder_first_ref[:, columns], decoder_second_ref[:, columns]
        )
        slots[1][:, columns] = new.astype(bf16)
        for which in (1, 4, 5):
            send(which, columns)

    grad = act_grad * slope_ref[...]
    pre_ref[...] = grad.astype(bf16)
    latent_grad = jnp.sum(grad, axis=1, keepdims=True)

    for columns in blocks(ENCODER_BLOCKS):
        grad = jnp.dot(pre_ref[...], tokens_ref[:, columns], preferred_element_type=f32)
        new, slots[2][:, columns], slots[3][:, columns] = adam_update(
            encoder_ref[:, columns], grad, encoder_first_ref[:, columns], encoder_second_ref[:, columns]
        )
        slots[0][:, columns] = new.astype(bf16)
        for which in (0, 2, 3):
            send(which, columns)
    total = turn(latent_grad)
    slots[6][...], slots[7][...], slots[8][...] = adam_update(
        encoder_bias_ref[...], total, latent_first_ref[...], latent_second_ref[...]
    )
    for which in range(6, 9):
        send(which)
    rows = errors_ref[...].astype(f32)
    while rows.shape[0] > own:
        half = rows.shape[0] // 2
        rows = rows[:half] + rows[half:]
    total = rows[0:1]
    for row in range(1, own):
        total = total + rows[row : row + 1]
    slots[9][...], slots[10][...], slots[11][...] = adam_update(
        decoder_bias_ref[...], total, feature_first_ref[...], feature_second_ref[...]
    )
    for which in range(9, 12):
        send(which)
    for which in range(12):
        pltpu.make_async_copy(slots[which], outs[which], sems.at[which]).wait()


def update(own, errors, prepared, encoder, decoder, *short):
    latents, features = encoder.shape
    count = errors.shape[0]
    shapes = [((latents, features), bf16)] * 2 + [((latents, features), f32)] * 4
    shapes += [((1, latents), f32)] * 3 + [((1, features), f32)] * 3
    return pl.pallas_call(
        functools.partial(update_kernel, own),
        in_specs=[VMEM_SPEC] * 18,
        out_specs=[ANY_SPEC] * 12,
        out_shape=[jax.ShapeDtypeStruct(*shape) for shape in shapes],
        scratch_shapes=[pltpu.VMEM(*shape) for shape in shapes]
        + [pltpu.VMEM((latents, count), bf16), pltpu.SemaphoreType.DMA((12,))],
        compiler_params=pltpu.CompilerParams(vmem_limit_bytes=24 * 2**20),
        cost_estimate=pl.CostEstimate(
            flops=6 * count * latents * features,
            bytes_accessed=40 * latents * features,
            transcendentals=4 * latents * features,
        ),
    )(*map(in_vmem, (errors, *prepared, encoder, decoder, *short)))


def local(
    devices,
    tokens,
    encoder_weight,
    encoder_bias,
    decoder_weight,
    decoder_bias,
    encoder_first,
    encoder_second,
    decoder_first,
    decoder_second,
    latent_first,
    latent_second,
    feature_first,
    feature_second,
):
    far = [1 << b for b in reversed(range(3, devices.bit_length() - 1))]
    near = (4, 2, 6)
    near_last = (2, 4, 6)
    near_sums = (2, 4, 6)
    own = tokens.shape[0]
    row = lambda array: array.reshape(1, -1)
    encoder_bias, latent_first, latent_second, decoder_bias, feature_first, feature_second = map(
        row, (encoder_bias, latent_first, latent_second, decoder_bias, feature_first, feature_second)
    )
    other = swap(tokens, far[0], devices)
    (column,) = load(tokens)
    mate_encoder = swap(encoder_weight, 1, devices)
    mate_decoder = swap(decoder_weight, 1, devices)
    mate_bias = swap(encoder_bias, 1, devices)
    encoder, decoder, bias = load(encoder_weight, decoder_weight, encoder_bias)
    column = lax.optimization_barrier(jnp.concatenate([column, other], axis=0))
    for bit in far[1:]:
        column = lax.optimization_barrier(jnp.concatenate([column, swap(column, bit, devices)], axis=0))
    rows = column.shape[0]
    blocks = {bits: swap(column, bits, devices) for bits in near}
    last_column = lax.optimization_barrier(jnp.concatenate([column] + [blocks[bits] for bits in near_last], axis=0))
    column = lax.optimization_barrier(jnp.concatenate([column] + [blocks[bits] for bits in near], axis=0))
    part, *sent = forward(column, encoder, mate_encoder, bias, mate_bias, decoder, mate_decoder)
    sent = dict(zip(near, sent))
    received = [swap(sent[bits], bits, devices) for bits in near_sums]
    moments = load(encoder_first, encoder_second, decoder_first, decoder_second)
    received, moments = lax.optimization_barrier((received, moments))
    for piece in received:
        part = part + piece.astype(f32)
    for level in reversed(range(len(far))):
        part = lax.reduce_precision(part, 8, 7)
        piece = part.astype(bf16)
        other = swap(piece, far[level], devices)
        size = own << level
        pieces = [other[start ^ size : (start ^ size) + size] for start in range(0, rows, size)]
        part = part + jnp.concatenate(pieces, axis=0).astype(f32)
    errors = (part + decoder_bias - column[:rows].astype(f32)).astype(bf16)
    column = last_column
    errors, column = lax.optimization_barrier((errors, column))
    received = [swap(errors, bits, devices) for bits in near_last]
    prepared = prepare(column, swap(column, 1, devices), encoder, bias, decoder)
    errors = lax.optimization_barrier(jnp.concatenate([errors] + received, axis=0))
    errors = jnp.concatenate([errors, swap(errors, 1, devices)], axis=0)
    out = update(
        own,
        errors,
        (*prepared, *moments),
        encoder,
        decoder,
        bias,
        latent_first,
        latent_second,
        decoder_bias,
        feature_first,
        feature_second,
    )
    new_encoder, new_decoder, enc_first, enc_second, dec_first, dec_second = out[:6]
    lat_new, lat_first, lat_second, feat_new, feat_first, feat_second = (array.reshape(-1) for array in out[6:])
    return (
        new_encoder,
        lat_new,
        new_decoder,
        feat_new,
        enc_first,
        enc_second,
        dec_first,
        dec_second,
        lat_first,
        lat_second,
        feat_first,
        feat_second,
    )


def solution(mesh):
    devices = mesh.shape["dict"]
    in_specs = (
        P(("groups", "dict"), None),
        P(("groups", "dict"), None),
        P(("groups", "dict")),
        P(("groups", "dict"), None),
        P("groups"),
        P(("groups", "dict"), None),
        P(("groups", "dict"), None),
        P(("groups", "dict"), None),
        P(("groups", "dict"), None),
        P(("groups", "dict")),
        P(("groups", "dict")),
        P("groups"),
        P("groups"),
    )
    out_specs = (
        P(("groups", "dict"), None),
        P(("groups", "dict")),
        P(("groups", "dict"), None),
        P("groups"),
        P(("groups", "dict"), None),
        P(("groups", "dict"), None),
        P(("groups", "dict"), None),
        P(("groups", "dict"), None),
        P(("groups", "dict")),
        P(("groups", "dict")),
        P("groups"),
        P("groups"),
    )

    def step(*args):
        return local(devices, *args)

    return jax.shard_map(step, mesh=mesh, in_specs=in_specs, out_specs=out_specs, check_vma=False)
```

```python
import functools

import jax
import jax.numpy as jnp
from jax import lax
from jax.experimental import pallas as pl
from jax.experimental.pallas import tpu as pltpu
from jax.sharding import PartitionSpec as P

STEP = 100


sharpness = 4.0
sparsity_coef = 0.3
first_decay = 0.9
second_decay = 0.999
learn_rate = 0.001
epsilon = 1e-08

f32 = jnp.float32
bf16 = jnp.bfloat16


def adam_update(param, grad, first, second):
    first_new = first_decay * first + (1.0 - first_decay) * grad
    second_new = second_decay * second + (1.0 - second_decay) * grad * grad
    first_corr = 1.0 - first_decay**STEP
    second_corr = 1.0 - second_decay**STEP
    square = second_new * (1.0 / second_corr)
    root = square * lax.rsqrt(square)
    change = (learn_rate / first_corr) * first_new / (root + epsilon)
    return (param.astype(f32) - change, first_new, second_new)


def softplus(x):
    return jnp.maximum(x, 0.0) + jnp.log1p(jnp.exp(-jnp.abs(x)))


def nt_dot(a, b):
    return lax.dot_general(a, b, (((1,), (1,)), ((), ())), preferred_element_type=f32)


def turn(vector):
    side = max(vector.shape)
    square = (side, side)
    diagonal = lax.broadcasted_iota(jnp.int32, square, 0) == lax.broadcasted_iota(jnp.int32, square, 1)
    axis = 1 if vector.shape[0] == 1 else 0
    return jnp.sum(jnp.where(diagonal, jnp.broadcast_to(vector, square), 0.0), axis=axis, keepdims=True)


def swap(x, bit, devices):
    return lax.ppermute(x, "dict", [(i, i ^ bit) for i in range(devices)])


def in_vmem(array):
    return pltpu.with_memory_space_constraint(array, pltpu.VMEM)


def in_hbm(array):
    return pltpu.with_memory_space_constraint(array, pltpu.HBM)


VMEM_SPEC = pl.BlockSpec(memory_space=pltpu.VMEM)
ANY_SPEC = pl.BlockSpec(memory_space=pl.ANY)


def load_kernel(*refs):
    count = len(refs) // 2
    copies = [pltpu.make_async_copy(refs[i], refs[count + i], refs[-1].at[i]) for i in range(count)]
    for copy in copies:
        copy.start()
    for copy in copies:
        copy.wait()


def load(*arrays):
    return pl.pallas_call(
        load_kernel,
        in_specs=[ANY_SPEC] * len(arrays),
        out_specs=[VMEM_SPEC] * len(arrays),
        out_shape=[pltpu.VMEM(array.shape, array.dtype) for array in arrays],
        scratch_shapes=[pltpu.SemaphoreType.DMA((len(arrays),))],
        compiler_params=pltpu.CompilerParams(vmem_limit_bytes=2**20),
        cost_estimate=pl.CostEstimate(
            flops=0, bytes_accessed=2 * sum(array.size * array.dtype.itemsize for array in arrays), transcendentals=0
        ),
    )(*map(in_hbm, arrays))


def forward_kernel(
    tokens_ref,
    encoder_ref,
    mate_encoder_ref,
    bias_ref,
    mate_bias_ref,
    decoder_ref,
    mate_decoder_ref,
    keep_ref,
    *send_refs,
):
    tokens = tokens_ref[...]

    def act(weight_ref, row_ref):
        pre = nt_dot(tokens, weight_ref[...]) + row_ref[...]
        return (softplus(sharpness * pre) / sharpness).astype(bf16)

    own = act(encoder_ref, bias_ref)
    mate = act(mate_encoder_ref, mate_bias_ref)
    rows = keep_ref.shape[0]
    width = 1024
    for start in range(0, keep_ref.shape[1], width):
        columns = pl.ds(start, width)
        part = jnp.dot(own, decoder_ref[:, columns], preferred_element_type=f32) + jnp.dot(
            mate, mate_decoder_ref[:, columns], preferred_element_type=f32
        )
        keep_ref[:, columns] = part[:rows]
        for quarter, send_ref in enumerate(send_refs, 1):
            send_ref[:, columns] = part[quarter * rows : (quarter + 1) * rows].astype(bf16)


def forward(tokens, encoder, mate_encoder, bias, mate_bias, decoder, mate_decoder):
    rows, features = tokens.shape[0] // 4, tokens.shape[1]
    latents = encoder.shape[0]
    return pl.pallas_call(
        forward_kernel,
        in_specs=[VMEM_SPEC] * 7,
        out_specs=[VMEM_SPEC] * 4,
        out_shape=[pltpu.VMEM((rows, features), f32)] + [pltpu.VMEM((rows, features), bf16)] * 3,
        compiler_params=pltpu.CompilerParams(vmem_limit_bytes=16 * 2**20),
        cost_estimate=pl.CostEstimate(
            flops=32 * rows * latents * features, bytes_accessed=8 * latents * features, transcendentals=16 * rows * latents
        ),
    )(*map(in_vmem, (tokens, encoder, mate_encoder, bias, mate_bias, decoder, mate_decoder)))


def prepare_kernel(
    tokens_ref, mate_tokens_ref, encoder_ref, bias_ref, decoder_ref, gathered_ref, slope_ref, act_ref, floor_ref, pull_ref
):
    tokens = jnp.concatenate([tokens_ref[...], mate_tokens_ref[...]], axis=0)
    gathered_ref[...] = tokens
    pre = nt_dot(encoder_ref[...], tokens) + turn(bias_ref[...])
    act = softplus(sharpness * pre) / sharpness
    slope_ref[...] = jax.nn.sigmoid(sharpness * pre)
    act_ref[...] = act.astype(bf16)
    decoder = decoder_ref[...].astype(f32)
    norms = jnp.sqrt(jnp.sum(decoder * decoder, axis=1, keepdims=True) + 1e-06)
    floor_ref[...] = sparsity_coef * norms
    pull_ref[...] = sparsity_coef * jnp.sum(act, axis=1, keepdims=True) / norms


def prepare(tokens, mate_tokens, encoder, bias, decoder):
    latents, features = encoder.shape
    count = 2 * tokens.shape[0]
    return pl.pallas_call(
        prepare_kernel,
        in_specs=[VMEM_SPEC] * 5,
        out_specs=[VMEM_SPEC] * 5,
        out_shape=[
            pltpu.VMEM((count, features), bf16),
            pltpu.VMEM((latents, count), f32),
            pltpu.VMEM((latents, count), bf16),
            pltpu.VMEM((latents, 1), f32),
            pltpu.VMEM((latents, 1), f32),
        ],
        compiler_params=pltpu.CompilerParams(vmem_limit_bytes=16 * 2**20),
        cost_estimate=pl.CostEstimate(
            flops=2 * count * latents * features, bytes_accessed=10 * latents * features, transcendentals=3 * count * latents
        ),
    )(*map(in_vmem, (tokens, mate_tokens, encoder, bias, decoder)))


DECODER_BLOCKS = (1,) * 8
ENCODER_BLOCKS = (1,) * 8


def update_kernel(
    own,
    errors_ref,
    tokens_ref,
    slope_ref,
    act_ref,
    floor_ref,
    pull_ref,
    encoder_first_ref,
    encoder_second_ref,
    decoder_first_ref,
    decoder_second_ref,
    encoder_ref,
    decoder_ref,
    encoder_bias_ref,
    latent_first_ref,
    latent_second_ref,
    decoder_bias_ref,
    feature_first_ref,
    feature_second_ref,
    *refs,
):
    outs, slots, (pre_ref, sems) = refs[:12], refs[12:24], refs[24:]
    features = encoder_ref.shape[1]

    def send(which, columns=slice(None)):
        pltpu.make_async_copy(slots[which].at[:, columns], outs[which].at[:, columns], sems.at[which]).start()

    def blocks(eighths):
        start = 0
        for count in eighths:
            width = features // 8 * count
            yield pl.ds(start, width)
            start += width

    act_grad = floor_ref[...]
    for columns in blocks(DECODER_BLOCKS):
        act_grad = act_grad + nt_dot(decoder_ref[:, columns], errors_ref[:, columns])
        weight = decoder_ref[:, columns].astype(f32)
        grad = jnp.dot(act_ref[...], errors_ref[:, columns], preferred_element_type=f32) + pull_ref[...] * weight
        new, slots[4][:, columns], slots[5][:, columns] = adam_update(
            weight, grad, decoder_first_ref[:, columns], decoder_second_ref[:, columns]
        )
        slots[1][:, columns] = new.astype(bf16)
        for which in (1, 4, 5):
            send(which, columns)

    grad = act_grad * slope_ref[...]
    pre_ref[...] = grad.astype(bf16)
    latent_grad = jnp.sum(grad, axis=1, keepdims=True)

    for columns in blocks(ENCODER_BLOCKS):
        grad = jnp.dot(pre_ref[...], tokens_ref[:, columns], preferred_element_type=f32)
        new, slots[2][:, columns], slots[3][:, columns] = adam_update(
            encoder_ref[:, columns], grad, encoder_first_ref[:, columns], encoder_second_ref[:, columns]
        )
        slots[0][:, columns] = new.astype(bf16)
        for which in (0, 2, 3):
            send(which, columns)
    total = turn(latent_grad)
    slots[6][...], slots[7][...], slots[8][...] = adam_update(
        encoder_bias_ref[...], total, latent_first_ref[...], latent_second_ref[...]
    )
    for which in range(6, 9):
        send(which)
    rows = errors_ref[...].astype(f32)
    while rows.shape[0] > own:
        half = rows.shape[0] // 2
        rows = rows[:half] + rows[half:]
    total = rows[0:1]
    for row in range(1, own):
        total = total + rows[row : row + 1]
    slots[9][...], slots[10][...], slots[11][...] = adam_update(
        decoder_bias_ref[...], total, feature_first_ref[...], feature_second_ref[...]
    )
    for which in range(9, 12):
        send(which)
    for which in range(12):
        pltpu.make_async_copy(slots[which], outs[which], sems.at[which]).wait()


def update(own, errors, prepared, encoder, decoder, *short):
    latents, features = encoder.shape
    count = errors.shape[0]
    shapes = [((latents, features), bf16)] * 2 + [((latents, features), f32)] * 4
    shapes += [((1, latents), f32)] * 3 + [((1, features), f32)] * 3
    return pl.pallas_call(
        functools.partial(update_kernel, own),
        in_specs=[VMEM_SPEC] * 18,
        out_specs=[ANY_SPEC] * 12,
        out_shape=[jax.ShapeDtypeStruct(*shape) for shape in shapes],
        scratch_shapes=[pltpu.VMEM(*shape) for shape in shapes]
        + [pltpu.VMEM((latents, count), bf16), pltpu.SemaphoreType.DMA((12,))],
        compiler_params=pltpu.CompilerParams(vmem_limit_bytes=24 * 2**20),
        cost_estimate=pl.CostEstimate(
            flops=6 * count * latents * features,
            bytes_accessed=40 * latents * features,
            transcendentals=4 * latents * features,
        ),
    )(*map(in_vmem, (errors, *prepared, encoder, decoder, *short)))


def local(
    devices,
    tokens,
    encoder_weight,
    encoder_bias,
    decoder_weight,
    decoder_bias,
    encoder_first,
    encoder_second,
    decoder_first,
    decoder_second,
    latent_first,
    latent_second,
    feature_first,
    feature_second,
):
    far = [1 << b for b in reversed(range(3, devices.bit_length() - 1))]
    near = (4, 2, 6)
    near_last = (2, 4, 6)
    near_sums = (2, 4, 6)
    own = tokens.shape[0]
    row = lambda array: array.reshape(1, -1)
    encoder_bias, latent_first, latent_second, decoder_bias, feature_first, feature_second = map(
        row, (encoder_bias, latent_first, latent_second, decoder_bias, feature_first, feature_second)
    )
    other = swap(tokens, far[0], devices)
    (column,) = load(tokens)
    mate_encoder = swap(encoder_weight, 1, devices)
    mate_decoder = swap(decoder_weight, 1, devices)
    mate_bias = swap(encoder_bias, 1, devices)
    encoder, decoder, bias = load(encoder_weight, decoder_weight, encoder_bias)
    column = lax.optimization_barrier(jnp.concatenate([column, other], axis=0))
    for bit in far[1:]:
        column = lax.optimization_barrier(jnp.concatenate([column, swap(column, bit, devices)], axis=0))
    rows = column.shape[0]
    blocks = {bits: swap(column, bits, devices) for bits in near}
    last_column = lax.optimization_barrier(jnp.concatenate([column] + [blocks[bits] for bits in near_last], axis=0))
    column = lax.optimization_barrier(jnp.concatenate([column] + [blocks[bits] for bits in near], axis=0))
    part, *sent = forward(column, encoder, mate_encoder, bias, mate_bias, decoder, mate_decoder)
    sent = dict(zip(near, sent))
    received = [swap(sent[bits], bits, devices) for bits in near_sums]
    moments = load(encoder_first, encoder_second, decoder_first, decoder_second)
    received, moments = lax.optimization_barrier((received, moments))
    for piece in received:
        part = part + piece.astype(f32)
    for level in reversed(range(len(far))):
        part = lax.reduce_precision(part, 8, 7)
        size = own << level
        low = part.astype(bf16)
        pieces = [low[start ^ size : (start ^ size) + size] for start in range(0, rows, size)]
        part = part + swap(jnp.concatenate(pieces, axis=0), far[level], devices).astype(f32)
    errors = (part + decoder_bias - column[:rows].astype(f32)).astype(bf16)
    column = last_column
    errors, column = lax.optimization_barrier((errors, column))
    received = [swap(errors, bits, devices) for bits in near_last]
    prepared = prepare(column, swap(column, 1, devices), encoder, bias, decoder)
    errors = lax.optimization_barrier(jnp.concatenate([errors] + received, axis=0))
    errors = jnp.concatenate([errors, swap(errors, 1, devices)], axis=0)
    out = update(
        own,
        errors,
        (*prepared, *moments),
        encoder,
        decoder,
        bias,
        latent_first,
        latent_second,
        decoder_bias,
        feature_first,
        feature_second,
    )
    new_encoder, new_decoder, enc_first, enc_second, dec_first, dec_second = out[:6]
    lat_new, lat_first, lat_second, feat_new, feat_first, feat_second = (array.reshape(-1) for array in out[6:])
    return (
        new_encoder,
        lat_new,
        new_decoder,
        feat_new,
        enc_first,
        enc_second,
        dec_first,
        dec_second,
        lat_first,
        lat_second,
        feat_first,
        feat_second,
    )


def solution(mesh):
    devices = mesh.shape["dict"]
    in_specs = (
        P(("groups", "dict"), None),
        P(("groups", "dict"), None),
        P(("groups", "dict")),
        P(("groups", "dict"), None),
        P("groups"),
        P(("groups", "dict"), None),
        P(("groups", "dict"), None),
        P(("groups", "dict"), None),
        P(("groups", "dict"), None),
        P(("groups", "dict")),
        P(("groups", "dict")),
        P("groups"),
        P("groups"),
    )
    out_specs = (
        P(("groups", "dict"), None),
        P(("groups", "dict")),
        P(("groups", "dict"), None),
        P("groups"),
        P(("groups", "dict"), None),
        P(("groups", "dict"), None),
        P(("groups", "dict"), None),
        P(("groups", "dict"), None),
        P(("groups", "dict")),
        P(("groups", "dict")),
        P("groups"),
        P("groups"),
    )

    def step(*args):
        return local(devices, *args)

    return jax.shard_map(step, mesh=mesh, in_specs=in_specs, out_specs=out_specs, check_vma=False)
```
